32 devices in a mesh: dp: 8 (over y, x, core), tensor: 4 (over z).
Axes of the slice: x: 2, y: 2, z: 4, core: 2. Of those that a mesh axis runs over, the one named last changes fastest.
Arguments:
- tokens: bfloat16 [4096, 768], P(('dp', 'tensor')), may hold values from -6 to 6
- doc_ids: int32 [4096], P('dp'), may hold values from 0 to 2, as said below
- expert_ids: int32 [4096, 1], P('dp'), may hold values from 0 to 3; in each aligned block of 512 rows (0 to 511, 512 to 1023, ...) at most 144 rows name the same one
- cotangent: bfloat16 [4096, 768], P(('dp', 'tensor')), may hold values from -6 to 6
- w_query: bfloat16 [768, 768], P('dp', 'tensor'), may hold values from -0.0546875 to 0.0546875
- w_key: bfloat16 [768, 768], P('dp', 'tensor'), may hold values from -0.21875 to 0.21875
- w_value: bfloat16 [768, 768], P('dp', 'tensor'), may hold values from -0.21875 to 0.21875
- w_attn_out: bfloat16 [768, 768], P('tensor', 'dp'), may hold values from -1.25 to 1.25
- gain_attn: float32 [768], replicated, may hold values from 0.5 to 1.5
- gain_expert: float32 [768], replicated, may hold values from 0.5 to 1.5
- rel_bias: float32 [32, 12], replicated, may hold values from -3 to 3
- w_router: bfloat16 [768, 4], P('dp'), may hold values from -0.15625 to 0.15625
- w_expert_in: bfloat16 [4, 768, 3072], P(None, 'dp', 'tensor'), may hold values from -0.21875 to 0.21875
- w_expert_out: bfloat16 [4, 3072, 768], P(None, 'tensor', 'dp'), may hold values from -0.4375 to 0.4375
Outputs:
- layer_out: bfloat16 [4096, 768], P(('dp', 'tensor'))
- grad_tokens: bfloat16 [4096, 768], P(('dp', 'tensor'))
- grad_query: float32 [768, 768], P('dp', 'tensor')
- grad_key: float32 [768, 768], P('dp', 'tensor')
- grad_value: float32 [768, 768], P('dp', 'tensor')
- grad_attn_out: float32 [768, 768], P('tensor', 'dp')
- grad_gain_attn: float32 [768], replicated
- grad_gain_expert: float32 [768], replicated
- grad_rel_bias: float32 [32, 12], replicated
- grad_router: float32 [768, 4], P('dp')
- grad_expert_in: float32 [4, 768, 3072], P(None, 'dp', 'tensor')
- grad_expert_out: float32 [4, 3072, 768], P(None, 'tensor', 'dp')
The draws below stay inside these ranges and needn't reach their ends.
Inputs may be any that keep to these rules, and one draw needn't show every extreme that they name: `doc_ids`: within each group of 512 rows the numbers never fall; every group has a document 1 that begins in the group's first fifth and ends in its last fifth, and some group holds document 1 alone over all its rows. `expert_ids`: among the 512 rows of one group at most 144 name the same expert.
All inputs are finite; a program needn't handle non-finite values.
Results may differ from the reference program's by a relative error of at most 0.014.
The reference program's roundings to bfloat16 on the way count: a program that leaves them out, or rounds other values in their place, can miss the bound.
Values may be sent and summed in bfloat16 or wider, within the bound.
A program may use at most 192 MiB of HBM per device.

```python
import math
import jax
import jax.numpy as jnp
import numpy as np
from jax import lax

D = 768
HEADS = 12
HEAD_DIM = 64
FF = 3072
BUCKETS = 32
MAX_DIST = 128
EXPERTS = 4
TOK_GRP = 512
TOKENS = 4096
CAPACITY = 144
N_DP = 8


def draw_doc_ids(key, part):
    key = jax.random.fold_in(key, 17)
    key_first, key_last, key_whole = jax.random.split(key, 3)
    reach_rows = max(TOK_GRP // 5, 2)
    first_end = jax.random.randint(key_first, (N_DP,), 1, reach_rows)
    last_start = TOK_GRP - jax.random.randint(key_last, (N_DP,), 1, reach_rows)
    whole_group = jax.random.randint(key_whole, (), 0, N_DP)
    single = jnp.arange(N_DP) == whole_group
    first_end = jnp.where(single, 0, first_end)
    last_start = jnp.where(single, TOK_GRP, last_start)
    positions = jnp.arange(TOK_GRP)
    doc_numbers = (positions[None, :] >= first_end[:, None]).astype(jnp.int32) + (positions[None, :] >= last_start[:, None]).astype(jnp.int32)
    return doc_numbers.reshape(N_DP * TOK_GRP)


def block_scale(own_key, shape, cuts, low, largest):
    def one(axis_at, shards_of):
        steps = jax.random.uniform(jax.random.fold_in(jax.random.fold_in(own_key, 6), axis_at), (shards_of,), jnp.float32, low / len(cuts), largest / len(cuts))
        return jnp.repeat(jnp.exp(steps), shape[axis_at] // shards_of).reshape((-1,) + (1,) * (len(shape) - axis_at - 1))

    gain = one(*cuts[0])
    for cut in cuts[1:]:
        gain = gain * one(*cut)
    return gain


def routed_block(stream_key, own, number, rows, number_of, top, most, slope):
    order = jax.random.permutation(stream_key, number_of)
    crowded, usual = portions_of(number_of, rows * top, most, slope, True), portions_of(number_of, rows * top, most, slope, False)
    places = jnp.arange(number_of)

    def named(tallies, turn):
        used = int((tallies > 0).sum())
        fixed = max(1, used // 4)
        moved = fixed + (places - fixed + turn * (used - fixed)) % max(1, number_of - fixed)
        return jnp.zeros((number_of,), jnp.int32).at[order[jnp.where(places < fixed, places, moved)]].set(jnp.asarray(tallies, jnp.int32))

    tallies = jnp.where(number % 4 == 0, named(crowded, number // 4), named(usual, number - number // 4 - 1))
    mixed = jax.random.permutation(jax.random.fold_in(own, 3), number_of)
    giver, taker = mixed[0:number_of // 2 * 2:2], mixed[1:number_of // 2 * 2:2]
    slack = jnp.minimum(tallies[giver] - 1, most - tallies[taker]) // 2
    slack = jnp.where((giver == order[0]) | (taker == order[0]) | (tallies[taker] == 0), 0, jnp.maximum(slack, 0))
    moved = jax.random.randint(jax.random.fold_in(own, 4), (number_of // 2,), 0, 1 << 20) % (slack + 1)
    tallies = tallies.at[giver].add(-moved).at[taker].add(moved)
    members = jnp.searchsorted(jnp.cumsum(tallies), jnp.arange(rows * top), side="right").astype(jnp.int32)
    listing = members.reshape(top, rows).T
    listing = listing[jax.random.permutation(jax.random.fold_in(own, 1), rows)]
    turn = jax.random.randint(jax.random.fold_in(own, 2), (rows, 1), 0, top)
    return jnp.take_along_axis(listing, (jnp.arange(top)[None, :] + turn) % top, axis=1)


def portions_of(amount, total, limit, slope, full):
    portions = [(1 << 20) // math.isqrt(grade ** slope) + 1 for grade in range(1, amount + 1)]
    largest = limit if full else min(limit, max(-(-total // amount), total * portions[0] // sum(portions)))
    least = 1 if total - largest >= amount - 1 else 0
    holding, surplus = [largest] + [least] * (amount - 1), total - largest - least * (amount - 1)
    while surplus > 0:
        free = [i for i in range(1, amount) if holding[i] < largest] or [i for i in range(1, amount) if holding[i] < limit]
        whole, left = sum([portions[i] for i in free]), surplus
        for i in free:
            addition = min(limit - holding[i], max(1, left * portions[i] // whole), surplus)
            holding[i] = holding[i] + addition
            surplus = surplus - addition
    return np.array(holding)


def bell_draw(key, extent, deviation, limit, cuts=(), held_as=jnp.bfloat16):
    array = jax.random.normal(key, extent, jnp.float32) * deviation
    if len(cuts) > 0:
        array = block_scale(key, extent, cuts, -0.22, 0.18) * array
    return jnp.clip(array, min=-limit, max=limit).astype(held_as)


def setup_inputs(seed: int = 0) -> dict:
    arg_keys = jax.random.split(jax.random.key(seed), 15)
    tokens = bell_draw(arg_keys[0], (TOKENS, D), 1.0, 6.0, ((0, 32),))
    doc_ids = draw_doc_ids(jax.random.fold_in(arg_keys[14], 71), 0)
    expert_ids_keys = jax.random.split(jax.random.fold_in(arg_keys[2], 1), TOKENS // TOK_GRP)
    expert_ids_turns = jax.random.permutation(jax.random.fold_in(arg_keys[2], 3), TOKENS // TOK_GRP)
    expert_ids = jax.vmap(lambda own, number: routed_block(jax.random.fold_in(arg_keys[2], 2), own, number, TOK_GRP, EXPERTS, 1, CAPACITY, 1))(expert_ids_keys, expert_ids_turns).reshape((TOKENS, 1))
    cotangent = bell_draw(arg_keys[3], (TOKENS, D), 1.0, 6.0, ((0, 32),))
    w_query = bell_draw(arg_keys[4], (D, D), (16 * D) ** -0.5, 0.0546875, ((0, 8), (1, 4)))
    w_key = bell_draw(arg_keys[5], (D, D), D ** -0.5, 0.21875, ((0, 8), (1, 4)))
    w_value = bell_draw(arg_keys[6], (D, D), D ** -0.5, 0.21875, ((0, 8), (1, 4)))
    w_attn_out = bell_draw(arg_keys[7], (D, D), (D // 32) ** -0.5, 1.25, ((0, 4), (1, 8)))
    gain_attn = jnp.clip(1.0 + 0.1 * jax.random.normal(arg_keys[8], (D,), jnp.float32), 0.5, 1.5)
    gain_expert = jnp.clip(1.0 + 0.1 * jax.random.normal(arg_keys[9], (D,), jnp.float32), 0.5, 1.5)
    rel_bias = bell_draw(arg_keys[10], (BUCKETS, HEADS), 1.0, 3.0, (), jnp.float32)
    w_router = bell_draw(arg_keys[11], (D, EXPERTS), (2 * D) ** -0.5, 0.15625, ((0, 8),))
    w_expert_in = bell_draw(arg_keys[12], (EXPERTS, D, FF), D ** -0.5, 0.21875, ((1, 8), (2, 4)))
    w_expert_out = bell_draw(arg_keys[13], (EXPERTS, FF, D), (FF // 16) ** -0.5, 0.4375, ((1, 4), (2, 8)))
    return {"tokens": tokens, "doc_ids": doc_ids, "expert_ids": expert_ids, "cotangent": cotangent, "w_query": w_query, "w_key": w_key, "w_value": w_value, "w_attn_out": w_attn_out, "gain_attn": gain_attn, "gain_expert": gain_expert, "rel_bias": rel_bias, "w_router": w_router, "w_expert_in": w_expert_in, "w_expert_out": w_expert_out}


norm_eps = 1e-06
masked_score = -1e+30
full_prec = lax.Precision.HIGHEST

@jax.custom_vjp
def low(v):
    return lax.optimization_barrier(v.astype(jnp.bfloat16)).astype(jnp.float32)

@jax.custom_vjp
def low_back(v):
    return v

def low_keep(v):
    return (low(v), None)

def low_pass(kept, grad):
    return (grad,)

def back_keep(v):
    return (v, None)

def back_low(kept, grad):
    return (low(grad),)
low.defvjp(low_keep, low_pass)
low_back.defvjp(back_keep, back_low)

def bucket_onehot(length, buckets, max_reach):
    half_count = buckets // 2
    exact_count = half_count // 2
    offset = np.arange(-(length - 1), length)
    distance = np.abs(offset)
    far_bucket = exact_count + (np.log(np.maximum(distance, 1) / exact_count) / np.log(max_reach / exact_count) * (half_count - exact_count)).astype(np.int64)
    far_bucket = np.minimum(far_bucket, half_count - 1)
    bucket = np.where(distance < exact_count, distance, far_bucket) + half_count * (offset > 0)
    return (bucket[:, None] == np.arange(buckets)[None, :]).astype(np.float32)

def rms_scale(values):
    return lax.rsqrt(lax.optimization_barrier(jnp.mean(values * values, axis=-1, keepdims=True)) + norm_eps)

def group_layer(hidden_in, doc_row, route_row, param_list):
    query_w, key_w, value_w, attn_out_w, gain_one, gain_two, bias_table, router_w, inner_w, outer_w = param_list
    rows_count = hidden_in.shape[0]
    normed = low(hidden_in * rms_scale(hidden_in) * gain_one)

    def heads_of(matrix):
        projected = low_back(low(jnp.dot(normed, matrix, precision=full_prec)))
        return projected.reshape(rows_count, HEADS, HEAD_DIM).transpose(1, 0, 2)
    queries = heads_of(query_w)
    keys_all = heads_of(key_w)
    values_all = heads_of(value_w)
    onehot = jnp.asarray(bucket_onehot(rows_count, BUCKETS, MAX_DIST))
    offsets = jnp.dot(onehot, bias_table, precision=full_prec)
    positions = jnp.arange(rows_count)
    offset_index = positions[None, :] - positions[:, None] + rows_count - 1
    bias_all = jnp.take(offsets.T, offset_index, axis=1)
    same_doc = doc_row[:, None] == doc_row[None, :]
    scores = jnp.einsum('hqd,hkd->hqk', queries, keys_all, precision=full_prec) + bias_all
    scores = low_back(jnp.where(same_doc[None], scores, masked_score))
    prob_all = low(jax.nn.softmax(scores, axis=-1))
    mixed_all = jnp.einsum('hqk,hkd->qhd', prob_all, values_all, precision=full_prec).reshape(rows_count, D)
    mixed_all = low_back(low(mixed_all))
    attn_all = low_back(jnp.dot(mixed_all, attn_out_w, precision=full_prec))
    middle = hidden_in + attn_all
    normed_two = low(middle * rms_scale(middle) * gain_two)
    logits = low_back(jnp.dot(normed_two, router_w, precision=full_prec))
    gate_probs = jax.nn.softmax(logits, axis=-1)
    chosen = route_row[:, None] == jnp.arange(EXPERTS)[None, :]
    gate_value = lax.optimization_barrier(jnp.sum(jnp.where(chosen, gate_probs, 0.0), axis=-1))
    chosen_int = chosen.astype(jnp.int32)
    slot_index = lax.optimization_barrier(jnp.sum(jnp.cumsum(chosen_int, axis=0) * chosen_int, axis=-1)) - 1
    slot_place = route_row * CAPACITY + slot_index
    dispatch = (slot_place[None, :] == jnp.arange(EXPERTS * CAPACITY)[:, None]).astype(hidden_in.dtype)
    buffer = jnp.dot(dispatch, normed_two, precision=full_prec).reshape(EXPERTS, CAPACITY, D)
    inner_pre = low_back(jnp.einsum('ecd,edf->ecf', buffer, inner_w, precision=full_prec))
    inner_act = low(jax.nn.gelu(inner_pre, approximate=True))
    expert_out = low_back(jnp.einsum('ecf,efd->ecd', inner_act, outer_w, precision=full_prec))
    returned = jnp.dot(dispatch.T, expert_out.reshape(EXPERTS * CAPACITY, D), precision=full_prec)
    return middle + gate_value[:, None] * returned

def reference(tokens, doc_ids, expert_ids, cotangent, w_query, w_key, w_value, w_attn_out, gain_attn, gain_expert, rel_bias, w_router, w_expert_in, w_expert_out):
    param_list = tuple((weight.astype(jnp.float32) for weight in (w_query, w_key, w_value, w_attn_out, gain_attn, gain_expert, rel_bias, w_router, w_expert_in, w_expert_out)))
    inputs = tokens.astype(jnp.float32).reshape(N_DP, TOK_GRP, D)
    docs_all = doc_ids.reshape(N_DP, TOK_GRP)
    routes_all = expert_ids.reshape(N_DP, TOK_GRP)

    def forward(inputs_in, params_in):

        def group_step(scan_carry, group_item):
            return (scan_carry, jax.checkpoint(group_layer)(group_item[0], group_item[1], group_item[2], params_in))
        unused, outputs = lax.scan(group_step, jnp.zeros((), jnp.float32), (inputs_in, docs_all, routes_all))
        return outputs
    outputs, pull_back = jax.vjp(forward, inputs, param_list)
    grad_in, grad_params = pull_back(cotangent.astype(jnp.float32).reshape(N_DP, TOK_GRP, D))
    return (outputs.reshape(TOKENS, D).astype(jnp.bfloat16), grad_in.reshape(TOKENS, D).astype(jnp.bfloat16), grad_params[0], grad_params[1], grad_params[2], grad_params[3], grad_params[4], grad_params[5], grad_params[6], grad_params[7], grad_params[8], grad_params[9])
```

```python
import functools

import jax
import jax.numpy as jnp
import numpy as np
from jax import lax
from jax.experimental import pallas as pl
from jax.experimental.pallas import tpu as pltpu
from jax.sharding import PartitionSpec as P

HEAD_DIM = 64
BUCKETS = 32
MAX_DIST = 128


norm_eps = 1e-06
masked_score = -1e30
block_rows_max = 512


def bucket_table(length, buckets, max_reach):
    half_count = buckets // 2
    exact_count = half_count // 2
    positions = np.arange(length)
    offset = positions[None, :] - positions[:, None]
    distance = np.abs(offset)
    far_bucket = exact_count + (
        np.log(np.maximum(distance, 1) / exact_count)
        / np.log(max_reach / exact_count)
        * (half_count - exact_count)
    ).astype(np.int64)
    far_bucket = np.minimum(far_bucket, half_count - 1)
    bucket = np.where(distance < exact_count, distance, far_bucket) + half_count * (offset > 0)
    return bucket.astype(np.int32)


def rms_scale(values):
    return lax.rsqrt(jnp.mean(values * values, axis=-1, keepdims=True) + norm_eps)


def gelu_tanh(values):
    return jax.nn.gelu(values, approximate=True)


def exchange_kernel(plan, sizes, *refs):
    count = len(plan)
    ins, outs = refs[:count], refs[count : 2 * count]
    send_sem, recv_sem, own_sem = refs[2 * count :]
    barrier = pltpu.get_barrier_semaphore()
    greeted = 0
    for axis, size in sizes:
        me = lax.axis_index(axis)
        for step in range(1, size):
            pl.semaphore_signal(
                barrier,
                inc=1,
                device_id={axis: lax.rem(me + step, size)},
                device_id_type=pl.DeviceIdType.MESH,
            )
        greeted += size - 1
    pl.semaphore_wait(barrier, greeted)
    size_of = dict(sizes)
    copies = []
    for step in range(1, max(size_of.values())):
        for num, (axis, kind) in enumerate(plan):
            size = size_of[axis]
            if step >= size:
                continue
            me = lax.axis_index(axis)
            peer = lax.rem(me + step, size)
            copy = pltpu.make_async_remote_copy(
                src_ref=ins[num] if kind == "gather" else ins[num].at[peer],
                dst_ref=outs[num].at[me],
                send_sem=send_sem.at[num, step],
                recv_sem=recv_sem.at[num, step],
                device_id={axis: peer},
                device_id_type=pl.DeviceIdType.MESH,
            )
            copy.start()
            copies.append(copy)
    for num, (axis, kind) in enumerate(plan):
        me = lax.axis_index(axis)
        own = pltpu.make_async_copy(
            ins[num] if kind == "gather" else ins[num].at[me], outs[num].at[me], own_sem.at[num]
        )
        own.start()
        copies.append(own)
    for copy in copies:
        copy.wait()


def exchange(ident, items):
    plan = tuple((axis, kind) for unused, axis, kind in items)
    axes = sorted({axis for axis, unused in plan})
    sizes = tuple((axis, lax.axis_size(axis)) for axis in axes)
    size_of = dict(sizes)
    shapes = [
        jax.ShapeDtypeStruct(
            ((size_of[axis],) + x.shape) if kind == "gather" else x.shape, x.dtype
        )
        for x, axis, kind in items
    ]
    most = max(size_of.values())
    return pl.pallas_call(
        functools.partial(exchange_kernel, plan, sizes),
        out_shape=shapes,
        in_specs=[pl.BlockSpec(memory_space=pl.ANY)] * len(items),
        out_specs=[pl.BlockSpec(memory_space=pl.ANY)] * len(items),
        scratch_shapes=[
            pltpu.SemaphoreType.DMA((len(items), most)),
            pltpu.SemaphoreType.DMA((len(items), most)),
            pltpu.SemaphoreType.DMA((len(items),)),
        ],
        compiler_params=pltpu.CompilerParams(collective_id=ident, has_side_effects=True),
    )(*[x for x, unused, unused2 in items])


def dot_nn(left, right):
    return jnp.dot(left, right, preferred_element_type=jnp.float32)


def dot_nt(left, right):
    return lax.dot_general(left, right, (((1,), (1,)), ((), ())), preferred_element_type=jnp.float32)


def dot_tn(left, right):
    return lax.dot_general(left, right, (((0,), (0,)), ((), ())), preferred_element_type=jnp.float32)


def sum_parts(parts):
    return jnp.sum(parts.astype(jnp.float32), axis=0)


def norm_backward(grad_out, inputs_in, scale_in, gain_vec):
    scaled = grad_out * gain_vec
    grad_in = scale_in * scaled - inputs_in * scale_in**3 * jnp.mean(
        scaled * inputs_in, axis=-1, keepdims=True
    )
    grad_gain = jnp.sum(grad_out * inputs_in * scale_in, axis=0)
    return (grad_in, grad_gain)


def block_scores(query_block, keys_all, rel_local, ids_block, doc_block, docs_all):
    raw_scores = jnp.einsum(
        "rhd,khd->hrk", query_block, keys_all, preferred_element_type=jnp.float32
    )
    bias_block = jnp.zeros(raw_scores.shape, jnp.float32)
    for bucket_num in range(rel_local.shape[0]):
        bias_block = jnp.where(
            (ids_block == bucket_num)[None], rel_local[bucket_num][:, None, None], bias_block
        )
    same_doc = doc_block[:, None] == docs_all[None, :]
    return jnp.where(same_doc[None], raw_scores + bias_block, masked_score)


def bucket_sums(grad_scores, ids_block, bucket_total):
    sums_list = [
        jnp.sum(jnp.where((ids_block == bucket_num)[None], grad_scores, 0.0), axis=(1, 2))
        for bucket_num in range(bucket_total)
    ]
    return jnp.stack(sums_list, axis=0)


def body(
    tokens,
    doc_ids,
    expert_ids,
    cotangent,
    w_query,
    w_key,
    w_value,
    w_attn_out,
    gain_attn,
    gain_expert,
    rel_bias,
    w_router,
    w_expert_in,
    w_expert_out,
):
    tensor_count = lax.axis_size("tensor")
    group_count = lax.axis_size("dp")
    local_rows = tokens.shape[0]
    group_rows = local_rows * tensor_count
    model_width = tokens.shape[1]
    width_share = model_width // group_count
    my_start = lax.axis_index("tensor") * local_rows
    expert_count = w_router.shape[1]
    serve_count = group_count // expert_count
    base_slots = 9 * group_rows // (8 * expert_count)
    capacity = (base_slots + serve_count - 1) // serve_count * serve_count
    slot_count = expert_count * capacity
    share_rows = capacity // serve_count
    share_pad = (share_rows + 15) // 16 * 16
    head_width = w_query.shape[1]
    head_count = head_width // HEAD_DIM
    bf = jnp.bfloat16
    sent_attn = jnp.concatenate(
        [
            w_query,
            w_key,
            w_value,
            w_attn_out.T,
            jnp.pad(w_router, ((0, 0), (0, 128 - expert_count))),
        ],
        axis=1,
    )
    sent_experts = jnp.repeat(
        jnp.stack([w_expert_in, w_expert_out.transpose(0, 2, 1)], axis=1), serve_count, axis=0
    )
    hidden_share = w_expert_in.shape[2]
    head_start = lax.axis_index("tensor") * head_count
    block_rows = min(block_rows_max, group_rows)
    block_count = group_rows // block_rows
    id_table = jnp.asarray(bucket_table(group_rows, BUCKETS, MAX_DIST))
    rel_local = lax.dynamic_slice_in_dim(rel_bias, head_start, head_count, 1)
    route_ids = expert_ids[:, 0]
    input_f = tokens.astype(jnp.float32)
    scale_one = rms_scale(input_f)
    sent_one = (input_f * scale_one * gain_attn).astype(bf)
    normed_parts, attn_parts, grad_parts = exchange(
        1,
        [(sent_one, "tensor", "gather"), (sent_attn, "dp", "gather"), (cotangent, "tensor", "gather")],
    )
    expert_parts = lax.all_to_all(sent_experts, "dp", split_axis=0, concat_axis=0, tiled=True)
    normed_one = normed_parts.reshape(group_rows, model_width)
    grad_full = grad_parts.reshape(group_rows, model_width)
    attn_full = attn_parts.reshape(model_width, sent_attn.shape[1])
    qkv_full = attn_full[:, : 3 * head_width]
    out_turned = attn_full[:, 3 * head_width : 4 * head_width]
    router_full = attn_full[:, 4 * head_width : 4 * head_width + expert_count]
    projected = dot_nn(normed_one, qkv_full).astype(bf)
    queries, keys_all, values_all = (
        projected[:, part * head_width : (part + 1) * head_width].reshape(
            group_rows, head_count, HEAD_DIM
        )
        for part in range(3)
    )
    query_blocks = queries.reshape(block_count, block_rows, head_count, HEAD_DIM)
    doc_blocks = doc_ids.reshape(block_count, block_rows)
    id_blocks = id_table.reshape(block_count, block_rows, group_rows)

    def attend(block_in):
        query_block, doc_block, ids_block = block_in
        scores = block_scores(query_block, keys_all, rel_local, ids_block, doc_block, doc_ids)
        top_score = jnp.max(scores, axis=-1, keepdims=True)
        exp_scores = jnp.exp(scores - top_score)
        exp_total = jnp.sum(exp_scores, axis=-1, keepdims=True)
        prob_bf = (exp_scores / exp_total).astype(jnp.bfloat16)
        mixed_block = jnp.einsum(
            "hrk,khd->rhd", prob_bf, values_all, preferred_element_type=jnp.float32
        )
        log_total = top_score[..., 0] + jnp.log(exp_total[..., 0])
        return (mixed_block.astype(jnp.bfloat16), log_total)

    mixed_blocks, log_totals = lax.map(attend, (query_blocks, doc_blocks, id_blocks))
    mixed_all = mixed_blocks.reshape(group_rows, head_count * HEAD_DIM)
    attn_sent = dot_nt(mixed_all, out_turned).astype(bf)
    (attn_back,) = exchange(
        2, [(attn_sent.reshape(tensor_count, local_rows, model_width), "tensor", "swap")]
    )
    middle = input_f + sum_parts(attn_back)
    scale_two = rms_scale(middle)
    normed_local = (middle * scale_two * gain_expert).astype(bf)
    (normed_two,) = exchange(3, [(normed_local, "tensor", "gather")])
    normed_two = normed_two.reshape(group_rows, model_width)
    logits = dot_nn(normed_two, router_full)
    gate_probs = jax.nn.softmax(logits, axis=-1)
    chosen = route_ids[:, None] == jnp.arange(expert_count)[None, :]
    gate_value = jnp.sum(jnp.where(chosen, gate_probs, 0.0), axis=-1)
    earlier = jnp.asarray(np.tril(np.ones((group_rows, group_rows), np.float32), -1), bf)
    counts = dot_nn(earlier, chosen.astype(bf))
    slot_index = jnp.sum(jnp.where(chosen, counts, 0.0), axis=-1).astype(jnp.int32)
    server = route_ids * serve_count + slot_index // share_rows
    slot_place = server * share_pad + slot_index % share_rows
    place = (
        slot_place[None, :] == jnp.arange(group_count * share_pad, dtype=jnp.int32)[:, None]
    ).astype(bf)
    grad_f = grad_full.astype(jnp.float32)
    gated = (gate_value[:, None] * grad_f).astype(bf)
    both = dot_nn(place, jnp.concatenate([normed_two, gated], axis=1)).astype(bf)
    (recv_both,) = exchange(
        4, [(both.reshape(group_count, share_pad, 2 * model_width), "dp", "swap")]
    )
    recv_both = recv_both.reshape(group_count * share_pad, 2 * model_width)
    rows_mine = recv_both[:, :model_width]
    grad_mine = recv_both[:, model_width:]
    inner_mine = expert_parts[:, 0].reshape(model_width, hidden_share)
    outer_mine = expert_parts[:, 1].reshape(model_width, hidden_share)
    inner_pre = dot_nn(rows_mine, inner_mine)
    inner_act, gelu_pull = jax.vjp(gelu_tanh, inner_pre)
    inner_act = inner_act.astype(bf)
    expert_part = dot_nt(inner_act, outer_mine).astype(bf)
    grad_pre = gelu_pull(dot_nn(grad_mine, outer_mine))[0].astype(bf)
    grad_rows = dot_nt(grad_pre, inner_mine).astype(bf)
    (back_both,) = exchange(
        5,
        [
            (
                jnp.concatenate([expert_part, grad_rows], axis=1).reshape(
                    group_count, share_pad, 2 * model_width
                ),
                "dp",
                "swap",
            )
        ],
    )
    inner_grad = dot_tn(rows_mine, grad_pre).astype(bf)
    outer_grad = dot_tn(grad_mine, inner_act).astype(bf)
    weight_back = lax.all_to_all(
        jnp.stack(
            [
                inner_grad.reshape(group_count, width_share, hidden_share),
                outer_grad.reshape(group_count, width_share, hidden_share),
            ],
            axis=1,
        ),
        "dp",
        split_axis=0,
        concat_axis=0,
        tiled=True,
    )
    weight_sum = jnp.sum(
        weight_back.reshape(
            expert_count, serve_count, 2, width_share, hidden_share
        ).astype(jnp.float32),
        axis=1,
    )
    inner_sum = weight_sum[:, 0]
    outer_sum = weight_sum[:, 1].transpose(0, 2, 1)
    returned = dot_tn(place, back_both.reshape(group_count * share_pad, 2 * model_width)).astype(bf)
    (row_back,) = exchange(
        6, [(returned.reshape(tensor_count, local_rows, 2 * model_width), "tensor", "swap")]
    )
    row_sum = sum_parts(row_back)
    expert_local = row_sum[:, :model_width]
    gate_local = lax.dynamic_slice_in_dim(gate_value, my_start, local_rows, 0)
    layer_out = (middle + gate_local[:, None] * expert_local).astype(bf)
    cot_local = cotangent.astype(jnp.float32)
    gate_grad = jnp.sum(cot_local * expert_local, axis=-1)
    probs_local = lax.dynamic_slice_in_dim(gate_probs, my_start, local_rows, 0)
    chosen_local = lax.dynamic_slice_in_dim(chosen.astype(jnp.float32), my_start, local_rows, 0)
    grad_logits = (probs_local * gate_grad[:, None] * (chosen_local - gate_local[:, None])).astype(
        jnp.bfloat16
    )
    grad_router_part = jnp.einsum(
        "qd,qe->de", normed_local, grad_logits, preferred_element_type=jnp.float32
    )
    router_term = jnp.einsum(
        "qe,de->qd", grad_logits, router_full, preferred_element_type=jnp.float32
    )
    grad_two_local = row_sum[:, model_width:] + router_term
    grad_mid, grad_gain_two = norm_backward(grad_two_local, middle, scale_two, gain_expert)
    grad_middle = cot_local + grad_mid
    (grad_mid_full,) = exchange(7, [(grad_middle.astype(bf), "tensor", "gather")])
    grad_mid_full = grad_mid_full.reshape(group_rows, model_width)
    grad_out_w = dot_tn(grad_mid_full, mixed_all)
    grad_mixed = dot_nn(grad_mid_full, out_turned).astype(bf)
    grad_mixed_blocks = grad_mixed.reshape(block_count, block_rows, head_count, HEAD_DIM)
    bucket_total = rel_bias.shape[0]

    def attend_back(carry_in, block_in):
        grad_keys, grad_values, bias_acc = carry_in
        query_block, doc_block, ids_block, log_total, grad_block = block_in
        scores = block_scores(query_block, keys_all, rel_local, ids_block, doc_block, doc_ids)
        probs_f = jnp.exp(scores - log_total[..., None])
        prob_bf = probs_f.astype(jnp.bfloat16)
        grad_probs = jnp.einsum(
            "rhd,khd->hrk", grad_block, values_all, preferred_element_type=jnp.float32
        )
        row_dot = jnp.sum(probs_f * grad_probs, axis=-1, keepdims=True)
        grad_scores = (probs_f * (grad_probs - row_dot)).astype(jnp.bfloat16)
        grad_query_block = jnp.einsum(
            "hrk,khd->rhd", grad_scores, keys_all, preferred_element_type=jnp.float32
        )
        grad_keys = grad_keys + jnp.einsum(
            "hrk,rhd->khd", grad_scores, query_block, preferred_element_type=jnp.float32
        )
        grad_values = grad_values + jnp.einsum(
            "hrk,rhd->khd", prob_bf, grad_block, preferred_element_type=jnp.float32
        )
        bias_acc = bias_acc + bucket_sums(grad_scores.astype(jnp.float32), ids_block, bucket_total)
        return ((grad_keys, grad_values, bias_acc), grad_query_block)

    zero_heads = jnp.zeros((group_rows, head_count, HEAD_DIM), jnp.float32)
    zero_bias = jnp.zeros((bucket_total, head_count), jnp.float32)
    final_carry, grad_query_blocks = lax.scan(
        attend_back,
        (zero_heads, zero_heads, zero_bias),
        (query_blocks, doc_blocks, id_blocks, log_totals, grad_mixed_blocks),
    )
    grad_keys, grad_values, grad_rel_local = final_carry
    grad_rel_full = lax.dynamic_update_slice_in_dim(
        jnp.zeros(rel_bias.shape, jnp.float32), grad_rel_local, head_start, 1
    )
    query_grad_bf = grad_query_blocks.reshape(group_rows, head_count * HEAD_DIM).astype(
        jnp.bfloat16
    )
    key_grad_bf = grad_keys.reshape(group_rows, head_count * HEAD_DIM).astype(jnp.bfloat16)
    value_grad_bf = grad_values.reshape(group_rows, head_count * HEAD_DIM).astype(jnp.bfloat16)
    grad_qkv = jnp.concatenate([query_grad_bf, key_grad_bf, value_grad_bf], axis=1)
    grad_one_sent = dot_nt(grad_qkv, qkv_full).astype(bf)
    (grad_one_back,) = exchange(
        8, [(grad_one_sent.reshape(tensor_count, local_rows, model_width), "tensor", "swap")]
    )
    grad_qkv_w = dot_tn(normed_one, grad_qkv)
    attn_grads = jnp.concatenate([grad_qkv_w, grad_out_w], axis=1).astype(bf)
    grad_one_local = sum_parts(grad_one_back)
    grad_in_norm, grad_gain_one = norm_backward(grad_one_local, input_f, scale_one, gain_attn)
    grad_tokens = (grad_middle + grad_in_norm).astype(bf)
    small = jnp.concatenate(
        [
            grad_gain_one,
            grad_gain_two,
            grad_rel_full.reshape(-1),
            grad_router_part.T.reshape(-1),
        ]
    )
    small_size = small.shape[0]
    small_rows = (small_size + 1023) // 1024 * 8
    small = jnp.pad(small, (0, small_rows * 128 - small_size)).reshape(small_rows, 128)
    (small_parts,) = exchange(9, [(small, "tensor", "gather")])
    small_parts, attn_back_parts = exchange(
        10,
        [
            (jnp.sum(small_parts, axis=0), "dp", "gather"),
            (attn_grads.reshape(group_count, width_share, 4 * head_width), "dp", "swap"),
        ],
    )
    small_sum = jnp.sum(small_parts, axis=0).reshape(-1)
    gain_one_sum = small_sum[:model_width]
    gain_two_sum = small_sum[model_width : 2 * model_width]
    rel_end = 2 * model_width + rel_bias.size
    rel_sum = small_sum[2 * model_width : rel_end].reshape(rel_bias.shape)
    router_whole = small_sum[rel_end : rel_end + expert_count * model_width].reshape(
        expert_count, model_width
    )
    router_sum = lax.dynamic_slice_in_dim(
        router_whole, lax.axis_index("dp") * width_share, width_share, 1
    ).T
    attn_sum = sum_parts(attn_back_parts)
    query_sum, key_sum, value_sum = (
        attn_sum[:, part * head_width : (part + 1) * head_width] for part in range(3)
    )
    out_sum = attn_sum[:, 3 * head_width :].T
    return (
        layer_out,
        grad_tokens,
        query_sum,
        key_sum,
        value_sum,
        out_sum,
        gain_one_sum,
        gain_two_sum,
        rel_sum,
        router_sum,
        inner_sum,
        outer_sum,
    )


def solution(mesh):
    return jax.shard_map(
        body,
        mesh=mesh,
        in_specs=(
            P(("dp", "tensor"), None),
            P("dp"),
            P("dp", None),
            P(("dp", "tensor"), None),
            P("dp", "tensor"),
            P("dp", "tensor"),
            P("dp", "tensor"),
            P("tensor", "dp"),
            P(),
            P(),
            P(),
            P("dp", None),
            P(None, "dp", "tensor"),
            P(None, "tensor", "dp"),
        ),
        out_specs=(
            P(("dp", "tensor"), None),
            P(("dp", "tensor"), None),
            P("dp", "tensor"),
            P("dp", "tensor"),
            P("dp", "tensor"),
            P("tensor", "dp"),
            P(),
            P(),
            P(),
            P("dp", None),
            P(None, "dp", "tensor"),
            P(None, "tensor", "dp"),
        ),
        check_vma=False,
    )
```

```python
import functools

import jax
import jax.numpy as jnp
import numpy as np
from jax import lax
from jax.experimental import pallas as pl
from jax.experimental.pallas import tpu as pltpu
from jax.sharding import PartitionSpec as P

HEAD_DIM = 64
BUCKETS = 32
MAX_DIST = 128


norm_eps = 1e-06
masked_score = -1e30


def bucket_table(length, buckets, max_reach):
    half_count = buckets // 2
    exact_count = half_count // 2
    positions = np.arange(length)
    offset = positions[None, :] - positions[:, None]
    distance = np.abs(offset)
    far_bucket = exact_count + (
        np.log(np.maximum(distance, 1) / exact_count)
        / np.log(max_reach / exact_count)
        * (half_count - exact_count)
    ).astype(np.int64)
    far_bucket = np.minimum(far_bucket, half_count - 1)
    bucket = np.where(distance < exact_count, distance, far_bucket) + half_count * (offset > 0)
    return bucket.astype(np.int32)


def rms_scale(values):
    return lax.rsqrt(jnp.mean(values * values, axis=-1, keepdims=True) + norm_eps)


def gelu_tanh(values):
    return jax.nn.gelu(values, approximate=True)


pieces = 4
vmem_bytes = 48 * 1024 * 1024


def greet_line(barrier, axis, size):
    me = lax.axis_index(axis)
    for side, there in ((1, me < size - 1), (-1, me > 0)):

        @pl.when(there)
        def greet(side=side):
            pl.semaphore_signal(
                barrier,
                inc=1,
                device_id={axis: me + side},
                device_id_type=pl.DeviceIdType.MESH,
            )

    return (me < size - 1).astype(jnp.int32) + (me > 0).astype(jnp.int32)


def line_gather(axis, size, x_ref, out_ref, send_sem, recv_sem):
    me = lax.axis_index(axis)
    rows = x_ref.shape[0] // pieces

    def hop(way, step, piece):
        side = 1 - 2 * way
        block = me - side * step
        part = pl.ds(piece * rows, rows)
        return pltpu.make_async_remote_copy(
            src_ref=x_ref.at[part] if step == 0 else out_ref.at[block, part],
            dst_ref=out_ref.at[block, part],
            send_sem=send_sem.at[way, step, piece],
            recv_sem=recv_sem.at[way, step, piece],
            device_id={axis: me + side},
            device_id_type=pl.DeviceIdType.MESH,
        )

    def arrival(way, step, piece):
        side = 1 - 2 * way
        block = me - side * (step + 1)
        part = pl.ds(piece * rows, rows)
        return pltpu.make_async_remote_copy(
            src_ref=x_ref.at[part],
            dst_ref=out_ref.at[block, part],
            send_sem=send_sem.at[way, step, piece],
            recv_sem=recv_sem.at[way, step, piece],
            device_id={axis: me + side},
            device_id_type=pl.DeviceIdType.MESH,
        )

    def sends(way, step):
        if way == 0:
            return (me < size - 1) & (me >= step)
        return (me > 0) & (me + step <= size - 1)

    def receives(way, step):
        if way == 0:
            return me >= step + 1
        return me + step + 1 <= size - 1

    for step in range(size):
        for piece in range(pieces):
            for way in range(2):
                if step > 0:

                    @pl.when(receives(way, step - 1))
                    def landed(way=way, step=step, piece=piece):
                        arrival(way, step - 1, piece).wait_recv()

                if step < size - 1:

                    @pl.when(sends(way, step))
                    def forward(way=way, step=step, piece=piece):
                        hop(way, step, piece).start()

    for step in range(size - 1):
        for piece in range(pieces):
            for way in range(2):

                @pl.when(sends(way, step))
                def gone(way=way, step=step, piece=piece):
                    hop(way, step, piece).wait_send()


def line_sum_kernel(axis, size, x_ref, out_ref, got, going, send_sem, recv_sem):
    me = lax.axis_index(axis)
    barrier = pltpu.get_barrier_semaphore()
    pl.semaphore_wait(barrier, greet_line(barrier, axis, size))
    rows = x_ref.shape[1] // pieces

    def hop(way, dest, piece):
        part = pl.ds(piece * rows, rows)
        return pltpu.make_async_remote_copy(
            src_ref=going.at[way, dest, part],
            dst_ref=got.at[way, dest, part],
            send_sem=send_sem.at[way, dest, piece],
            recv_sem=recv_sem.at[way, dest, piece],
            device_id={axis: me + 1 - 2 * way},
            device_id_type=pl.DeviceIdType.MESH,
        )

    def before(way, dest):
        return me < dest if way == 0 else me > dest

    def first(way):
        return me == 0 if way == 0 else me == size - 1

    for order in range(size - 1):
        for piece in range(pieces):
            for way in range(2):
                dest = size - 1 - order if way == 0 else order
                part = pl.ds(piece * rows, rows)

                @pl.when(before(way, dest) & first(way))
                def begin(way=way, dest=dest, part=part):
                    going[way, dest, part] = x_ref[dest, part]

                @pl.when(before(way, dest) & jnp.logical_not(first(way)))
                def add(way=way, dest=dest, part=part, piece=piece):
                    hop(way, dest, piece).wait_recv()
                    going[way, dest, part] = (
                        x_ref[dest, part].astype(jnp.float32)
                        + got[way, dest, part].astype(jnp.float32)
                    ).astype(jnp.bfloat16)

                @pl.when(before(way, dest))
                def send(way=way, dest=dest, piece=piece):
                    hop(way, dest, piece).start()

    out_ref[...] = x_ref[me].astype(jnp.float32)
    for way in range(2):

        @pl.when(jnp.logical_not(first(way)))
        def finish(way=way):
            for piece in range(pieces):
                hop(way, me, piece).wait_recv()
            out_ref[...] += got[way, me].astype(jnp.float32)

    for dest in range(size):
        for piece in range(pieces):
            for way in range(2):

                @pl.when(before(way, dest))
                def gone(way=way, dest=dest, piece=piece):
                    hop(way, dest, piece).wait_send()


def line_sum(ident, x, axis):
    size = lax.axis_size(axis)
    block = pl.BlockSpec(memory_space=pltpu.VMEM)
    return pl.pallas_call(
        functools.partial(line_sum_kernel, axis, size),
        out_shape=jax.ShapeDtypeStruct(x.shape[1:], jnp.float32),
        in_specs=[block],
        out_specs=block,
        scratch_shapes=[
            pltpu.VMEM((2,) + x.shape, x.dtype),
            pltpu.VMEM((2,) + x.shape, x.dtype),
            pltpu.SemaphoreType.DMA((2, size, pieces)),
            pltpu.SemaphoreType.DMA((2, size, pieces)),
        ],
        compiler_params=pltpu.CompilerParams(
            collective_id=ident, has_side_effects=True, vmem_limit_bytes=vmem_bytes
        ),
    )(x)


def attend_kernel(head_width, normed_ref, weights_ref, base_ref, doc_col, doc_row, proj_ref, prob_ref, mixed_ref, sent_ref, bias):
    rows = normed_ref.shape[0]
    proj_ref[...] = dot_nn(normed_ref[...], weights_ref[:, : 3 * head_width]).astype(jnp.bfloat16)
    same = doc_col[...] == doc_row[...]
    mixed = []
    for head in range(head_width // HEAD_DIM):
        query, key, value = (
            proj_ref[:, part * head_width + head * HEAD_DIM : part * head_width + (head + 1) * HEAD_DIM]
            for part in range(3)
        )
        base = base_ref[head]
        for block in range(rows // 8):
            turned = base if block == 0 else pltpu.roll(base, 8 * block, 1)
            bias[8 * block : 8 * block + 8, :] = turned[:, :rows]
        scores = jnp.where(same, dot_nt(query, key) + bias[...], masked_score)
        exps = jnp.exp(scores - jnp.max(scores, axis=-1, keepdims=True))
        probs = exps / jnp.sum(exps, axis=-1, keepdims=True)
        prob_ref[head] = probs
        mixed.append(dot_nn(probs.astype(jnp.bfloat16), value).astype(jnp.bfloat16))
    mixed_ref[...] = jnp.concatenate(mixed, axis=1)
    sent_ref[...] = dot_nt(
        mixed_ref[...], weights_ref[:, 3 * head_width : 4 * head_width]
    ).astype(jnp.bfloat16)


def attend_back_kernel(head_width, grad_ref, weights_ref, proj_ref, prob_ref, grads_ref, sent_ref, diag_ref, wide):
    rows = grad_ref.shape[0]
    grad_mixed = dot_nn(
        grad_ref[...], weights_ref[:, 3 * head_width : 4 * head_width]
    ).astype(jnp.bfloat16)
    grads = [[], [], []]
    wide[:, rows:] = jnp.zeros((rows, rows), jnp.float32)
    for head in range(head_width // HEAD_DIM):
        query, key, value = (
            proj_ref[:, part * head_width + head * HEAD_DIM : part * head_width + (head + 1) * HEAD_DIM]
            for part in range(3)
        )
        grad_head = grad_mixed[:, head * HEAD_DIM : (head + 1) * HEAD_DIM]
        probs = prob_ref[head]
        grad_probs = dot_nt(grad_head, value)
        row_dot = jnp.sum(probs * grad_probs, axis=-1, keepdims=True)
        grad_scores = (probs * (grad_probs - row_dot)).astype(jnp.bfloat16)
        grads[0].append(dot_nn(grad_scores, key).astype(jnp.bfloat16))
        grads[1].append(dot_tn(grad_scores, query).astype(jnp.bfloat16))
        grads[2].append(dot_tn(probs.astype(jnp.bfloat16), grad_head).astype(jnp.bfloat16))
        wide[:, :rows] = grad_scores.astype(jnp.float32)
        total = wide[0:8, :]
        for block in range(1, rows // 8):
            total = total + pltpu.roll(wide[8 * block : 8 * block + 8, :], 2 * rows - 8 * block, 1)
        diag_ref[head] = total
    grads_ref[...] = jnp.concatenate(grads[0] + grads[1] + grads[2], axis=1)
    sent_ref[...] = dot_nt(grads_ref[...], weights_ref[:, : 3 * head_width]).astype(jnp.bfloat16)


def bucket_onehot(length):
    spread = np.arange(2 * length)[None, :] - np.arange(8)[:, None]
    spread = (spread + length) % (2 * length) - length
    table = bucket_table(length, BUCKETS, MAX_DIST)
    line = np.concatenate([table[:, 0][::-1], table[0, 1:]])
    picked = line[np.clip(spread + length - 1, 0, 2 * length - 2)]
    return (picked[None] == np.arange(BUCKETS)[:, None, None]).astype(np.float32)


def exchange_kernel(plan, sizes, *refs):
    count = len(plan)
    ins, outs = refs[:count], refs[count : 2 * count]
    send_sem, recv_sem, own_sem, line_send, line_recv = refs[2 * count :]
    barrier = pltpu.get_barrier_semaphore()
    greeted = 0
    direct = {axis for axis, kind in plan if kind != "line"}
    for axis, size in sizes:
        me = lax.axis_index(axis)
        if axis not in direct:
            greeted += greet_line(barrier, axis, size)
            continue
        for step in range(1, size):
            pl.semaphore_signal(
                barrier,
                inc=1,
                device_id={axis: lax.rem(me + step, size)},
                device_id_type=pl.DeviceIdType.MESH,
            )
        greeted += size - 1
    pl.semaphore_wait(barrier, greeted)
    size_of = dict(sizes)
    copies = []
    for step in range(1, max(size_of.values())):
        for num, (axis, kind) in enumerate(plan):
            size = size_of[axis]
            if step >= size or kind == "line":
                continue
            me = lax.axis_index(axis)
            peer = lax.rem(me + step, size)
            copy = pltpu.make_async_remote_copy(
                src_ref=ins[num] if kind == "gather" else ins[num].at[peer],
                dst_ref=outs[num].at[me],
                send_sem=send_sem.at[num, step],
                recv_sem=recv_sem.at[num, step],
                device_id={axis: peer},
                device_id_type=pl.DeviceIdType.MESH,
            )
            copy.start()
            copies.append(copy)
    for num, (axis, kind) in enumerate(plan):
        me = lax.axis_index(axis)
        own = pltpu.make_async_copy(
            ins[num].at[me] if kind == "swap" else ins[num], outs[num].at[me], own_sem.at[num]
        )
        own.start()
        copies.append(own)
    for num, (axis, kind) in enumerate(plan):
        if kind == "line":
            line_gather(
                axis, size_of[axis], ins[num], outs[num], line_send.at[num], line_recv.at[num]
            )
    for copy in copies:
        copy.wait()


def exchange(ident, items):
    plan = tuple((axis, kind) for unused, axis, kind in items)
    axes = sorted({axis for axis, unused in plan})
    sizes = tuple((axis, lax.axis_size(axis)) for axis in axes)
    size_of = dict(sizes)
    shapes = [
        jax.ShapeDtypeStruct(
            ((size_of[axis],) + x.shape) if kind != "swap" else x.shape, x.dtype
        )
        for x, axis, kind in items
    ]
    most = max(size_of.values())
    return pl.pallas_call(
        functools.partial(exchange_kernel, plan, sizes),
        out_shape=shapes,
        in_specs=[pl.BlockSpec(memory_space=pl.ANY)] * len(items),
        out_specs=[pl.BlockSpec(memory_space=pl.ANY)] * len(items),
        scratch_shapes=[
            pltpu.SemaphoreType.DMA((len(items), most)),
            pltpu.SemaphoreType.DMA((len(items), most)),
            pltpu.SemaphoreType.DMA((len(items),)),
            pltpu.SemaphoreType.DMA((len(items), 2, most, pieces)),
            pltpu.SemaphoreType.DMA((len(items), 2, most, pieces)),
        ],
        compiler_params=pltpu.CompilerParams(collective_id=ident, has_side_effects=True),
    )(*[x for x, unused, unused2 in items])


def dot_nn(left, right):
    return jnp.dot(left, right, preferred_element_type=jnp.float32)


def dot_nt(left, right):
    return lax.dot_general(left, right, (((1,), (1,)), ((), ())), preferred_element_type=jnp.float32)


def dot_tn(left, right):
    return lax.dot_general(left, right, (((0,), (0,)), ((), ())), preferred_element_type=jnp.float32)


def sum_parts(parts):
    return jnp.sum(parts.astype(jnp.float32), axis=0)


def norm_backward(grad_out, inputs_in, scale_in, gain_vec):
    scaled = grad_out * gain_vec
    grad_in = scale_in * scaled - inputs_in * scale_in**3 * jnp.mean(
        scaled * inputs_in, axis=-1, keepdims=True
    )
    grad_gain = jnp.sum(grad_out * inputs_in * scale_in, axis=0)
    return (grad_in, grad_gain)


def body(
    tokens,
    doc_ids,
    expert_ids,
    cotangent,
    w_query,
    w_key,
    w_value,
    w_attn_out,
    gain_attn,
    gain_expert,
    rel_bias,
    w_router,
    w_expert_in,
    w_expert_out,
):
    tensor_count = lax.axis_size("tensor")
    group_count = lax.axis_size("dp")
    local_rows = tokens.shape[0]
    group_rows = local_rows * tensor_count
    model_width = tokens.shape[1]
    width_share = model_width // group_count
    my_start = lax.axis_index("tensor") * local_rows
    expert_count = w_router.shape[1]
    serve_count = group_count // expert_count
    base_slots = 9 * group_rows // (8 * expert_count)
    capacity = (base_slots + serve_count - 1) // serve_count * serve_count
    slot_count = expert_count * capacity
    share_rows = capacity // serve_count
    share_pad = (share_rows + 15) // 16 * 16
    head_width = w_query.shape[1]
    head_count = head_width // HEAD_DIM
    bf = jnp.bfloat16
    sent_attn = jnp.concatenate(
        [
            w_query,
            w_key,
            w_value,
            w_attn_out.T,
            jnp.pad(w_router, ((0, 0), (0, 128 - expert_count))),
        ],
        axis=1,
    )
    sent_experts = jnp.repeat(
        jnp.stack([w_expert_in, w_expert_out.transpose(0, 2, 1)], axis=1), serve_count, axis=0
    )
    hidden_share = w_expert_in.shape[2]
    head_start = lax.axis_index("tensor") * head_count
    rel_local = lax.dynamic_slice_in_dim(rel_bias, head_start, head_count, 1)
    route_ids = expert_ids[:, 0]
    input_f = tokens.astype(jnp.float32)
    scale_one = rms_scale(input_f)
    sent_one = (input_f * scale_one * gain_attn).astype(bf)
    normed_parts, attn_parts = exchange(
        1, [(sent_one, "tensor", "line"), (sent_attn, "dp", "gather")]
    )
    expert_parts = lax.all_to_all(sent_experts, "dp", split_axis=0, concat_axis=0, tiled=True)
    normed_one = normed_parts.reshape(group_rows, model_width)
    attn_full = attn_parts.reshape(model_width, sent_attn.shape[1])
    router_full = attn_full[:, 4 * head_width : 4 * head_width + expert_count]
    onehot = jnp.asarray(bucket_onehot(group_rows))
    rel_base = jnp.einsum(
        "bh,brt->hrt", rel_local, onehot, precision=lax.Precision.HIGHEST
    )
    vmem_block = pl.BlockSpec(memory_space=pltpu.VMEM)
    projected, probs, mixed_all, attn_sent = pl.pallas_call(
        functools.partial(attend_kernel, head_width),
        out_shape=[
            jax.ShapeDtypeStruct((group_rows, 3 * head_width), bf),
            jax.ShapeDtypeStruct((head_count, group_rows, group_rows), jnp.float32),
            jax.ShapeDtypeStruct((group_rows, head_width), bf),
            jax.ShapeDtypeStruct((group_rows, model_width), bf),
        ],
        in_specs=[vmem_block] * 5,
        out_specs=[vmem_block] * 4,
        scratch_shapes=[pltpu.VMEM((group_rows, group_rows), jnp.float32)],
        compiler_params=pltpu.CompilerParams(vmem_limit_bytes=vmem_bytes),
    )(normed_one, attn_full, rel_base, doc_ids[:, None], doc_ids[None, :])
    attn_sum_local = line_sum(
        2, attn_sent.reshape(tensor_count, local_rows, model_width), "tensor"
    )
    middle = input_f + attn_sum_local
    scale_two = rms_scale(middle)
    normed_local = (middle * scale_two * gain_expert).astype(bf)
    normed_two, grad_full = exchange(
        3, [(normed_local, "tensor", "line"), (cotangent, "tensor", "line")]
    )
    normed_two = normed_two.reshape(group_rows, model_width)
    grad_full = grad_full.reshape(group_rows, model_width)
    logits = dot_nn(normed_two, router_full)
    gate_probs = jax.nn.softmax(logits, axis=-1)
    chosen = route_ids[:, None] == jnp.arange(expert_count)[None, :]
    gate_value = jnp.sum(jnp.where(chosen, gate_probs, 0.0), axis=-1)
    earlier = jnp.asarray(np.tril(np.ones((group_rows, group_rows), np.float32), -1), bf)
    counts = dot_nn(earlier, chosen.astype(bf))
    slot_index = jnp.sum(jnp.where(chosen, counts, 0.0), axis=-1).astype(jnp.int32)
    server = route_ids * serve_count + slot_index // share_rows
    slot_place = server * share_pad + slot_index % share_rows
    place = (
        slot_place[None, :] == jnp.arange(group_count * share_pad, dtype=jnp.int32)[:, None]
    ).astype(bf)
    grad_f = grad_full.astype(jnp.float32)
    gated = (gate_value[:, None] * grad_f).astype(bf)
    both = dot_nn(place, jnp.concatenate([normed_two, gated], axis=1)).astype(bf)
    (recv_both,) = exchange(
        4, [(both.reshape(group_count, share_pad, 2 * model_width), "dp", "swap")]
    )
    recv_both = recv_both.reshape(group_count * share_pad, 2 * model_width)
    rows_mine = recv_both[:, :model_width]
    grad_mine = recv_both[:, model_width:]
    inner_mine = expert_parts[:, 0].reshape(model_width, hidden_share)
    outer_mine = expert_parts[:, 1].reshape(model_width, hidden_share)
    inner_pre = dot_nn(rows_mine, inner_mine)
    inner_act, gelu_pull = jax.vjp(gelu_tanh, inner_pre)
    inner_act = inner_act.astype(bf)
    expert_part = dot_nt(inner_act, outer_mine).astype(bf)
    grad_pre = gelu_pull(dot_nn(grad_mine, outer_mine))[0].astype(bf)
    grad_rows = dot_nt(grad_pre, inner_mine).astype(bf)
    (back_both,) = exchange(
        5,
        [
            (
                jnp.concatenate([expert_part, grad_rows], axis=1).reshape(
                    group_count, share_pad, 2 * model_width
                ),
                "dp",
                "swap",
            )
        ],
    )
    inner_grad = dot_tn(rows_mine, grad_pre).astype(bf)
    outer_grad = dot_tn(grad_mine, inner_act).astype(bf)
    weight_back = lax.all_to_all(
        jnp.stack(
            [
                inner_grad.reshape(group_count, width_share, hidden_share),
                outer_grad.reshape(group_count, width_share, hidden_share),
            ],
            axis=1,
        ),
        "dp",
        split_axis=0,
        concat_axis=0,
        tiled=True,
    )
    weight_sum = jnp.sum(
        weight_back.reshape(
            expert_count, serve_count, 2, width_share, hidden_share
        ).astype(jnp.float32),
        axis=1,
    )
    inner_sum = weight_sum[:, 0]
    outer_sum = weight_sum[:, 1].transpose(0, 2, 1)
    returned = dot_tn(place, back_both.reshape(group_count * share_pad, 2 * model_width)).astype(bf)
    row_sum = line_sum(6, returned.reshape(tensor_count, local_rows, 2 * model_width), "tensor")
    expert_local = row_sum[:, :model_width]
    gate_local = lax.dynamic_slice_in_dim(gate_value, my_start, local_rows, 0)
    layer_out = (middle + gate_local[:, None] * expert_local).astype(bf)
    cot_local = cotangent.astype(jnp.float32)
    gate_grad = jnp.sum(cot_local * expert_local, axis=-1)
    probs_local = lax.dynamic_slice_in_dim(gate_probs, my_start, local_rows, 0)
    chosen_local = lax.dynamic_slice_in_dim(chosen.astype(jnp.float32), my_start, local_rows, 0)
    grad_logits = (probs_local * gate_grad[:, None] * (chosen_local - gate_local[:, None])).astype(
        jnp.bfloat16
    )
    grad_router_part = jnp.einsum(
        "qd,qe->de", normed_local, grad_logits, preferred_element_type=jnp.float32
    )
    router_term = jnp.einsum(
        "qe,de->qd", grad_logits, router_full, preferred_element_type=jnp.float32
    )
    grad_two_local = row_sum[:, model_width:] + router_term
    grad_mid, grad_gain_two = norm_backward(grad_two_local, middle, scale_two, gain_expert)
    grad_middle = cot_local + grad_mid
    (grad_mid_full,) = exchange(7, [(grad_middle.astype(bf), "tensor", "line")])
    grad_mid_full = grad_mid_full.reshape(group_rows, model_width)
    grad_out_w = dot_tn(grad_mid_full, mixed_all)
    grad_qkv, grad_one_sent, diagonals = pl.pallas_call(
        functools.partial(attend_back_kernel, head_width),
        out_shape=[
            jax.ShapeDtypeStruct((group_rows, 3 * head_width), bf),
            jax.ShapeDtypeStruct((group_rows, model_width), bf),
            jax.ShapeDtypeStruct((head_count, 8, 2 * group_rows), jnp.float32),
        ],
        in_specs=[vmem_block] * 4,
        out_specs=[vmem_block] * 3,
        scratch_shapes=[pltpu.VMEM((group_rows, 2 * group_rows), jnp.float32)],
        compiler_params=pltpu.CompilerParams(vmem_limit_bytes=vmem_bytes),
    )(grad_mid_full, attn_full, projected, probs)
    grad_rel_local = jnp.einsum(
        "hrt,brt->bh", diagonals, onehot, precision=lax.Precision.HIGHEST
    )
    grad_rel_full = lax.dynamic_update_slice_in_dim(
        jnp.zeros(rel_bias.shape, jnp.float32), grad_rel_local, head_start, 1
    )
    grad_one_local = line_sum(
        8, grad_one_sent.reshape(tensor_count, local_rows, model_width), "tensor"
    )
    grad_qkv_w = dot_tn(normed_one, grad_qkv)
    attn_grads = jnp.concatenate([grad_qkv_w, grad_out_w], axis=1).astype(bf)
    grad_in_norm, grad_gain_one = norm_backward(grad_one_local, input_f, scale_one, gain_attn)
    grad_tokens = (grad_middle + grad_in_norm).astype(bf)
    small = jnp.concatenate(
        [
            grad_gain_one,
            grad_gain_two,
            grad_rel_full.reshape(-1),
            grad_router_part.T.reshape(-1),
        ]
    )
    small_size = small.shape[0]
    small_rows = (small_size + 1023) // 1024 * 8
    small = jnp.pad(small, (0, small_rows * 128 - small_size)).reshape(small_rows, 128)
    (small_parts,) = exchange(9, [(small, "tensor", "gather")])
    small_parts, attn_back_parts = exchange(
        10,
        [
            (jnp.sum(small_parts, axis=0), "dp", "gather"),
            (attn_grads.reshape(group_count, width_share, 4 * head_width), "dp", "swap"),
        ],
    )
    small_sum = jnp.sum(small_parts, axis=0).reshape(-1)
    gain_one_sum = small_sum[:model_width]
    gain_two_sum = small_sum[model_width : 2 * model_width]
    rel_end = 2 * model_width + rel_bias.size
    rel_sum = small_sum[2 * model_width : rel_end].reshape(rel_bias.shape)
    router_whole = small_sum[rel_end : rel_end + expert_count * model_width].reshape(
        expert_count, model_width
    )
    router_sum = lax.dynamic_slice_in_dim(
        router_whole, lax.axis_index("dp") * width_share, width_share, 1
    ).T
    attn_sum = sum_parts(attn_back_parts)
    query_sum, key_sum, value_sum = (
        attn_sum[:, part * head_width : (part + 1) * head_width] for part in range(3)
    )
    out_sum = attn_sum[:, 3 * head_width :].T
    return (
        layer_out,
        grad_tokens,
        query_sum,
        key_sum,
        value_sum,
        out_sum,
        gain_one_sum,
        gain_two_sum,
        rel_sum,
        router_sum,
        inner_sum,
        outer_sum,
    )


def solution(mesh):
    return jax.shard_map(
        body,
        mesh=mesh,
        in_specs=(
            P(("dp", "tensor"), None),
            P("dp"),
            P("dp", None),
            P(("dp", "tensor"), None),
            P("dp", "tensor"),
            P("dp", "tensor"),
            P("dp", "tensor"),
            P("tensor", "dp"),
            P(),
            P(),
            P(),
            P("dp", None),
            P(None, "dp", "tensor"),
            P(None, "tensor", "dp"),
        ),
        out_specs=(
            P(("dp", "tensor"), None),
            P(("dp", "tensor"), None),
            P("dp", "tensor"),
            P("dp", "tensor"),
            P("dp", "tensor"),
            P("tensor", "dp"),
            P(),
            P(),
            P(),
            P("dp", None),
            P(None, "dp", "tensor"),
            P(None, "tensor", "dp"),
        ),
        check_vma=False,
    )
```

```python
import functools

import jax
import jax.numpy as jnp
import numpy as np
from jax import lax
from jax.experimental import pallas as pl
from jax.experimental.pallas import tpu as pltpu
from jax.sharding import PartitionSpec as P

HEAD_DIM = 64
BUCKETS = 32
MAX_DIST = 128


norm_eps = 1e-06
masked_score = -1e30


def bucket_table(length, buckets, max_reach):
    half_count = buckets // 2
    exact_count = half_count // 2
    positions = np.arange(length)
    offset = positions[None, :] - positions[:, None]
    distance = np.abs(offset)
    far_bucket = exact_count + (
        np.log(np.maximum(distance, 1) / exact_count)
        / np.log(max_reach / exact_count)
        * (half_count - exact_count)
    ).astype(np.int64)
    far_bucket = np.minimum(far_bucket, half_count - 1)
    bucket = np.where(distance < exact_count, distance, far_bucket) + half_count * (offset > 0)
    return bucket.astype(np.int32)


def rms_scale(values):
    return lax.rsqrt(jnp.mean(values * values, axis=-1, keepdims=True) + norm_eps)


def gelu_tanh(values):
    return jax.nn.gelu(values, approximate=True)


pieces = 4
vmem_bytes = 48 * 1024 * 1024


def greet_line(barrier, axis, size):
    me = lax.axis_index(axis)
    for side, there in ((1, me < size - 1), (-1, me > 0)):

        @pl.when(there)
        def greet(side=side):
            pl.semaphore_signal(
                barrier,
                inc=1,
                device_id={axis: me + side},
                device_id_type=pl.DeviceIdType.MESH,
            )

    return (me < size - 1).astype(jnp.int32) + (me > 0).astype(jnp.int32)


def line_gather(axis, size, x_ref, out_ref, send_sem, recv_sem):
    me = lax.axis_index(axis)
    rows = x_ref.shape[0] // pieces

    def hop(way, step, piece):
        side = 1 - 2 * way
        block = me - side * step
        part = pl.ds(piece * rows, rows)
        return pltpu.make_async_remote_copy(
            src_ref=x_ref.at[part] if step == 0 else out_ref.at[block, part],
            dst_ref=out_ref.at[block, part],
            send_sem=send_sem.at[way, step, piece],
            recv_sem=recv_sem.at[way, step, piece],
            device_id={axis: me + side},
            device_id_type=pl.DeviceIdType.MESH,
        )

    def arrival(way, step, piece):
        side = 1 - 2 * way
        block = me - side * (step + 1)
        part = pl.ds(piece * rows, rows)
        return pltpu.make_async_remote_copy(
            src_ref=x_ref.at[part],
            dst_ref=out_ref.at[block, part],
            send_sem=send_sem.at[way, step, piece],
            recv_sem=recv_sem.at[way, step, piece],
            device_id={axis: me + side},
            device_id_type=pl.DeviceIdType.MESH,
        )

    def sends(way, step):
        if way == 0:
            return (me < size - 1) & (me >= step)
        return (me > 0) & (me + step <= size - 1)

    def receives(way, step):
        if way == 0:
            return me >= step + 1
        return me + step + 1 <= size - 1

    for step in range(size):
        for piece in range(pieces):
            for way in range(2):
                if step > 0:

                    @pl.when(receives(way, step - 1))
                    def landed(way=way, step=step, piece=piece):
                        arrival(way, step - 1, piece).wait_recv()

                if step < size - 1:

                    @pl.when(sends(way, step))
                    def forward(way=way, step=step, piece=piece):
                        hop(way, step, piece).start()

    for step in range(size - 1):
        for piece in range(pieces):
            for way in range(2):

                @pl.when(sends(way, step))
                def gone(way=way, step=step, piece=piece):
                    hop(way, step, piece).wait_send()


def greet_direct(barrier, axis, size):
    me = lax.axis_index(axis)
    for step in range(1, size):
        pl.semaphore_signal(
            barrier,
            inc=1,
            device_id={axis: lax.rem(me + step, size)},
            device_id_type=pl.DeviceIdType.MESH,
        )
    return size - 1


def start_swap(axis, size, x_ref, out_ref, send_sem, recv_sem):
    me = lax.axis_index(axis)
    copies = []
    for step in range(1, size):
        peer = lax.rem(me + step, size)
        copy = pltpu.make_async_remote_copy(
            src_ref=x_ref.at[peer],
            dst_ref=out_ref.at[me],
            send_sem=send_sem.at[step],
            recv_sem=recv_sem.at[step],
            device_id={axis: peer},
            device_id_type=pl.DeviceIdType.MESH,
        )
        copy.start()
        copies.append(copy)
    own = pltpu.make_async_copy(x_ref.at[me], out_ref.at[me], send_sem.at[0])
    own.start()
    return copies + [own]


def line_sum_kernel(axis, size, beside, *refs):
    x_ref = refs[0]
    if beside:
        other_ref, out_ref, other_out, got, going, send_sem, recv_sem, swap_send, swap_recv = refs[1:]
    else:
        out_ref, got, going, send_sem, recv_sem = refs[1:]
    me = lax.axis_index(axis)
    barrier = pltpu.get_barrier_semaphore()
    greeted = greet_line(barrier, axis, size)
    if beside:
        greeted += greet_direct(barrier, *beside)
    pl.semaphore_wait(barrier, greeted)
    rows = x_ref.shape[1] // pieces
    far = (me >= size // 2).astype(jnp.int32)

    def hop(way, dest, piece):
        part = pl.ds(piece * rows, rows)
        return pltpu.make_async_remote_copy(
            src_ref=going.at[way, dest, part],
            dst_ref=got.at[way, dest, part],
            send_sem=send_sem.at[way, dest, piece],
            recv_sem=recv_sem.at[way, dest, piece],
            device_id={axis: me + 1 - 2 * way},
            device_id_type=pl.DeviceIdType.MESH,
        )

    def before(way, dest):
        return (1 - 2 * way) * (dest - me) > 0

    def first(way):
        return me == (size - 1) * way

    copies = []
    for turn in range(2):
        way = far if turn == 0 else 1 - far
        for order in range(size - 1):
            dest = (size - 1 - order) * (1 - way) + order * way
            for piece in range(pieces):
                part = pl.ds(piece * rows, rows)

                @pl.when(before(way, dest) & first(way))
                def begin(way=way, dest=dest, part=part):
                    going[way, dest, part] = x_ref[dest, part]

                @pl.when(before(way, dest) & jnp.logical_not(first(way)))
                def add(way=way, dest=dest, part=part, piece=piece):
                    hop(way, dest, piece).wait_recv()
                    going[way, dest, part] = (
                        x_ref[dest, part].astype(jnp.float32)
                        + got[way, dest, part].astype(jnp.float32)
                    ).astype(jnp.bfloat16)

                @pl.when(before(way, dest))
                def send(way=way, dest=dest, piece=piece):
                    hop(way, dest, piece).start()

        if beside and turn == 0:
            copies = start_swap(*beside, other_ref, other_out, swap_send, swap_recv)

    out_ref[...] = x_ref[me].astype(jnp.float32)
    for way in range(2):

        @pl.when(jnp.logical_not(first(way)))
        def finish(way=way):
            for piece in range(pieces):
                hop(way, me, piece).wait_recv()
            out_ref[...] += got[way, me].astype(jnp.float32)

    for dest in range(size):
        for piece in range(pieces):
            for way in range(2):

                @pl.when(before(way, dest))
                def gone(way=way, dest=dest, piece=piece):
                    hop(way, dest, piece).wait_send()

    for copy in copies:
        copy.wait()


def line_sum(ident, x, axis, other=None, other_axis=None):
    size = lax.axis_size(axis)
    block = pl.BlockSpec(memory_space=pltpu.VMEM)
    place = pl.BlockSpec(memory_space=pl.ANY)
    out_shape = [jax.ShapeDtypeStruct(x.shape[1:], jnp.float32)]
    scratch = [
        pltpu.VMEM((2,) + x.shape, x.dtype),
        pltpu.VMEM((2,) + x.shape, x.dtype),
        pltpu.SemaphoreType.DMA((2, size, pieces)),
        pltpu.SemaphoreType.DMA((2, size, pieces)),
    ]
    beside = None
    extra = []
    if other is not None:
        beside = (other_axis, lax.axis_size(other_axis))
        extra = [other]
        out_shape.append(jax.ShapeDtypeStruct(other.shape, other.dtype))
        scratch += [pltpu.SemaphoreType.DMA((beside[1],)), pltpu.SemaphoreType.DMA((beside[1],))]
    return pl.pallas_call(
        functools.partial(line_sum_kernel, axis, size, beside),
        out_shape=out_shape,
        in_specs=[block] + [place] * len(extra),
        out_specs=[block] + [place] * len(extra),
        scratch_shapes=scratch,
        compiler_params=pltpu.CompilerParams(
            collective_id=ident, has_side_effects=True, vmem_limit_bytes=vmem_bytes
        ),
    )(x, *extra)


def attend_kernel(head_width, normed_ref, weights_ref, base_ref, doc_col, doc_row, proj_ref, prob_ref, mixed_ref, sent_ref, bias):
    rows = normed_ref.shape[0]
    proj_ref[...] = dot_nn(normed_ref[...], weights_ref[:, : 3 * head_width]).astype(jnp.bfloat16)
    same = doc_col[...] == doc_row[...]
    mixed = []
    for head in range(head_width // HEAD_DIM):
        query, key, value = (
            proj_ref[:, part * head_width + head * HEAD_DIM : part * head_width + (head + 1) * HEAD_DIM]
            for part in range(3)
        )
        base = base_ref[head]
        for block in range(rows // 8):
            turned = base if block == 0 else pltpu.roll(base, 8 * block, 1)
            bias[8 * block : 8 * block + 8, :] = turned[:, :rows]
        scores = jnp.where(same, dot_nt(query, key) + bias[...], masked_score)
        exps = jnp.exp(scores - jnp.max(scores, axis=-1, keepdims=True))
        probs = exps / jnp.sum(exps, axis=-1, keepdims=True)
        prob_ref[head] = probs
        mixed.append(dot_nn(probs.astype(jnp.bfloat16), value).astype(jnp.bfloat16))
    mixed_ref[...] = jnp.concatenate(mixed, axis=1)
    sent_ref[...] = dot_nt(
        mixed_ref[...], weights_ref[:, 3 * head_width : 4 * head_width]
    ).astype(jnp.bfloat16)


def attend_back_kernel(head_width, grad_ref, weights_ref, proj_ref, prob_ref, grads_ref, sent_ref, diag_ref, wide):
    rows = grad_ref.shape[0]
    grad_mixed = dot_nn(
        grad_ref[...], weights_ref[:, 3 * head_width : 4 * head_width]
    ).astype(jnp.bfloat16)
    grads = [[], [], []]
    wide[:, rows:] = jnp.zeros((rows, rows), jnp.float32)
    for head in range(head_width // HEAD_DIM):
        query, key, value = (
            proj_ref[:, part * head_width + head * HEAD_DIM : part * head_width + (head + 1) * HEAD_DIM]
            for part in range(3)
        )
        grad_head = grad_mixed[:, head * HEAD_DIM : (head + 1) * HEAD_DIM]
        probs = prob_ref[head]
        grad_probs = dot_nt(grad_head, value)
        row_dot = jnp.sum(probs * grad_probs, axis=-1, keepdims=True)
        grad_scores = (probs * (grad_probs - row_dot)).astype(jnp.bfloat16)
        grads[0].append(dot_nn(grad_scores, key).astype(jnp.bfloat16))
        grads[1].append(dot_tn(grad_scores, query).astype(jnp.bfloat16))
        grads[2].append(dot_tn(probs.astype(jnp.bfloat16), grad_head).astype(jnp.bfloat16))
        wide[:, :rows] = grad_scores.astype(jnp.float32)
        total = wide[0:8, :]
        for block in range(1, rows // 8):
            total = total + pltpu.roll(wide[8 * block : 8 * block + 8, :], 2 * rows - 8 * block, 1)
        diag_ref[head] = total
    grads_ref[...] = jnp.concatenate(grads[0] + grads[1] + grads[2], axis=1)
    sent_ref[...] = dot_nt(grads_ref[...], weights_ref[:, : 3 * head_width]).astype(jnp.bfloat16)


def bucket_onehot(length):
    spread = np.arange(2 * length)[None, :] - np.arange(8)[:, None]
    spread = (spread + length) % (2 * length) - length
    table = bucket_table(length, BUCKETS, MAX_DIST)
    line = np.concatenate([table[:, 0][::-1], table[0, 1:]])
    picked = line[np.clip(spread + length - 1, 0, 2 * length - 2)]
    return (picked[None] == np.arange(BUCKETS)[:, None, None]).astype(np.float32)


def exchange_kernel(plan, sizes, *refs):
    count = len(plan)
    ins, outs = refs[:count], refs[count : 2 * count]
    send_sem, recv_sem, own_sem, line_send, line_recv = refs[2 * count :]
    barrier = pltpu.get_barrier_semaphore()
    greeted = 0
    direct = {axis for axis, kind in plan if kind != "line"}
    for axis, size in sizes:
        me = lax.axis_index(axis)
        if axis not in direct:
            greeted += greet_line(barrier, axis, size)
            continue
        for step in range(1, size):
            pl.semaphore_signal(
                barrier,
                inc=1,
                device_id={axis: lax.rem(me + step, size)},
                device_id_type=pl.DeviceIdType.MESH,
            )
        greeted += size - 1
    pl.semaphore_wait(barrier, greeted)
    size_of = dict(sizes)
    copies = []
    for step in range(1, max(size_of.values())):
        for num, (axis, kind) in enumerate(plan):
            size = size_of[axis]
            if step >= size or kind == "line":
                continue
            me = lax.axis_index(axis)
            peer = lax.rem(me + step, size)
            copy = pltpu.make_async_remote_copy(
                src_ref=ins[num] if kind == "gather" else ins[num].at[peer],
                dst_ref=outs[num].at[me],
                send_sem=send_sem.at[num, step],
                recv_sem=recv_sem.at[num, step],
                device_id={axis: peer},
                device_id_type=pl.DeviceIdType.MESH,
            )
            copy.start()
            copies.append(copy)
    for num, (axis, kind) in enumerate(plan):
        me = lax.axis_index(axis)
        own = pltpu.make_async_copy(
            ins[num].at[me] if kind == "swap" else ins[num], outs[num].at[me], own_sem.at[num]
        )
        own.start()
        copies.append(own)
    for num, (axis, kind) in enumerate(plan):
        if kind == "line":
            line_gather(
                axis, size_of[axis], ins[num], outs[num], line_send.at[num], line_recv.at[num]
            )
    for copy in copies:
        copy.wait()


def exchange(ident, items):
    plan = tuple((axis, kind) for unused, axis, kind in items)
    axes = sorted({axis for axis, unused in plan})
    sizes = tuple((axis, lax.axis_size(axis)) for axis in axes)
    size_of = dict(sizes)
    shapes = [
        jax.ShapeDtypeStruct(
            ((size_of[axis],) + x.shape) if kind != "swap" else x.shape, x.dtype
        )
        for x, axis, kind in items
    ]
    most = max(size_of.values())
    return pl.pallas_call(
        functools.partial(exchange_kernel, plan, sizes),
        out_shape=shapes,
        in_specs=[pl.BlockSpec(memory_space=pl.ANY)] * len(items),
        out_specs=[pl.BlockSpec(memory_space=pl.ANY)] * len(items),
        scratch_shapes=[
            pltpu.SemaphoreType.DMA((len(items), most)),
            pltpu.SemaphoreType.DMA((len(items), most)),
            pltpu.SemaphoreType.DMA((len(items),)),
            pltpu.SemaphoreType.DMA((len(items), 2, most, pieces)),
            pltpu.SemaphoreType.DMA((len(items), 2, most, pieces)),
        ],
        compiler_params=pltpu.CompilerParams(collective_id=ident, has_side_effects=True),
    )(*[x for x, unused, unused2 in items])


def dot_nn(left, right):
    return jnp.dot(left, right, preferred_element_type=jnp.float32)


def dot_nt(left, right):
    return lax.dot_general(left, right, (((1,), (1,)), ((), ())), preferred_element_type=jnp.float32)


def dot_tn(left, right):
    return lax.dot_general(left, right, (((0,), (0,)), ((), ())), preferred_element_type=jnp.float32)


def sum_parts(parts):
    return jnp.sum(parts.astype(jnp.float32), axis=0)


def norm_backward(grad_out, inputs_in, scale_in, gain_vec):
    scaled = grad_out * gain_vec
    grad_in = scale_in * scaled - inputs_in * scale_in**3 * jnp.mean(
        scaled * inputs_in, axis=-1, keepdims=True
    )
    grad_gain = jnp.sum(grad_out * inputs_in * scale_in, axis=0)
    return (grad_in, grad_gain)


def body(
    tokens,
    doc_ids,
    expert_ids,
    cotangent,
    w_query,
    w_key,
    w_value,
    w_attn_out,
    gain_attn,
    gain_expert,
    rel_bias,
    w_router,
    w_expert_in,
    w_expert_out,
):
    tensor_count = lax.axis_size("tensor")
    group_count = lax.axis_size("dp")
    local_rows = tokens.shape[0]
    group_rows = local_rows * tensor_count
    model_width = tokens.shape[1]
    width_share = model_width // group_count
    my_start = lax.axis_index("tensor") * local_rows
    expert_count = w_router.shape[1]
    serve_count = group_count // expert_count
    base_slots = 9 * group_rows // (8 * expert_count)
    capacity = (base_slots + serve_count - 1) // serve_count * serve_count
    slot_count = expert_count * capacity
    share_rows = capacity // serve_count
    share_pad = (share_rows + 15) // 16 * 16
    head_width = w_query.shape[1]
    head_count = head_width // HEAD_DIM
    bf = jnp.bfloat16
    sent_attn = jnp.concatenate(
        [
            w_query,
            w_key,
            w_value,
            w_attn_out.T,
            jnp.pad(w_router, ((0, 0), (0, 128 - expert_count))),
        ],
        axis=1,
    )
    sent_experts = jnp.repeat(
        jnp.stack([w_expert_in, w_expert_out.transpose(0, 2, 1)], axis=1), serve_count, axis=0
    )
    hidden_share = w_expert_in.shape[2]
    head_start = lax.axis_index("tensor") * head_count
    rel_local = lax.dynamic_slice_in_dim(rel_bias, head_start, head_count, 1)
    route_ids = expert_ids[:, 0]
    input_f = tokens.astype(jnp.float32)
    scale_one = rms_scale(input_f)
    sent_one = (input_f * scale_one * gain_attn).astype(bf)
    normed_parts, attn_parts, grad_full = exchange(
        1,
        [
            (sent_one, "tensor", "line"),
            (sent_attn, "dp", "gather"),
            (cotangent, "tensor", "line"),
        ],
    )
    grad_full = grad_full.reshape(group_rows, model_width)
    sent_experts, normed_parts = lax.optimization_barrier((sent_experts, normed_parts))
    expert_parts = lax.all_to_all(sent_experts, "dp", split_axis=0, concat_axis=0, tiled=True)
    normed_one = normed_parts.reshape(group_rows, model_width)
    attn_full = attn_parts.reshape(model_width, sent_attn.shape[1])
    router_full = attn_full[:, 4 * head_width : 4 * head_width + expert_count]
    onehot = jnp.asarray(bucket_onehot(group_rows))
    rel_base = jnp.einsum(
        "bh,brt->hrt", rel_local, onehot, precision=lax.Precision.HIGHEST
    )
    vmem_block = pl.BlockSpec(memory_space=pltpu.VMEM)
    projected, probs, mixed_all, attn_sent = pl.pallas_call(
        functools.partial(attend_kernel, head_width),
        out_shape=[
            jax.ShapeDtypeStruct((group_rows, 3 * head_width), bf),
            jax.ShapeDtypeStruct((head_count, group_rows, group_rows), jnp.float32),
            jax.ShapeDtypeStruct((group_rows, head_width), bf),
            jax.ShapeDtypeStruct((group_rows, model_width), bf),
        ],
        in_specs=[vmem_block] * 5,
        out_specs=[vmem_block] * 4,
        scratch_shapes=[pltpu.VMEM((group_rows, group_rows), jnp.float32)],
        compiler_params=pltpu.CompilerParams(vmem_limit_bytes=vmem_bytes),
    )(normed_one, attn_full, rel_base, doc_ids[:, None], doc_ids[None, :])
    (attn_sum_local,) = line_sum(
        2, attn_sent.reshape(tensor_count, local_rows, model_width), "tensor"
    )
    chosen = route_ids[:, None] == jnp.arange(expert_count)[None, :]
    earlier = jnp.asarray(np.tril(np.ones((group_rows, group_rows), np.float32), -1), bf)
    counts = dot_nn(earlier, chosen.astype(bf))
    slot_index = jnp.sum(jnp.where(chosen, counts, 0.0), axis=-1).astype(jnp.int32)
    server = route_ids * serve_count + slot_index // share_rows
    slot_place = server * share_pad + slot_index % share_rows
    place = (
        slot_place[None, :] == jnp.arange(group_count * share_pad, dtype=jnp.int32)[:, None]
    ).astype(bf)
    grad_slots = dot_nn(place, grad_full).astype(bf)
    middle = input_f + attn_sum_local
    scale_two = rms_scale(middle)
    normed_local = (middle * scale_two * gain_expert).astype(bf)
    normed_two, recv_grad = exchange(
        3,
        [
            (normed_local, "tensor", "line"),
            (grad_slots.reshape(group_count, share_pad, model_width), "dp", "swap"),
        ],
    )
    normed_two = normed_two.reshape(group_rows, model_width)
    logits = dot_nn(normed_two, router_full)
    gate_probs = jax.nn.softmax(logits, axis=-1)
    gate_value = jnp.sum(jnp.where(chosen, gate_probs, 0.0), axis=-1)
    gate_slots = jnp.sum(jnp.where(place > 0, gate_value[None, :], 0.0), axis=1)
    sent_rows = dot_nn(place, normed_two).astype(bf)
    recv_rows, recv_gate = exchange(
        4,
        [
            (sent_rows.reshape(group_count, share_pad, model_width), "dp", "swap"),
            (gate_slots.reshape(group_count, 1, share_pad), "dp", "swap"),
        ],
    )
    rows_mine = recv_rows.reshape(group_count * share_pad, model_width)
    grad_mine = (
        (recv_gate.reshape(group_count, share_pad, 1) * recv_grad.astype(jnp.float32))
        .astype(bf)
        .reshape(group_count * share_pad, model_width)
    )
    inner_mine = expert_parts[:, 0].reshape(model_width, hidden_share)
    outer_mine = expert_parts[:, 1].reshape(model_width, hidden_share)
    inner_pre = dot_nn(rows_mine, inner_mine)
    inner_act, gelu_pull = jax.vjp(gelu_tanh, inner_pre)
    inner_act = inner_act.astype(bf)
    expert_part = dot_nt(inner_act, outer_mine).astype(bf)
    grad_pre = gelu_pull(dot_nn(grad_mine, outer_mine))[0].astype(bf)
    grad_rows = dot_nt(grad_pre, inner_mine).astype(bf)
    (back_rows,) = exchange(
        5, [(expert_part.reshape(group_count, share_pad, model_width), "dp", "swap")]
    )
    returned = dot_tn(place, back_rows.reshape(group_count * share_pad, model_width)).astype(bf)
    expert_local, back_grads = line_sum(
        6,
        returned.reshape(tensor_count, local_rows, model_width),
        "tensor",
        grad_rows.reshape(group_count, share_pad, model_width),
        "dp",
    )
    grads_returned = dot_tn(
        place, back_grads.reshape(group_count * share_pad, model_width)
    ).astype(bf)
    (slots_local,) = line_sum(
        11, grads_returned.reshape(tensor_count, local_rows, model_width), "tensor"
    )
    inner_grad = dot_tn(rows_mine, grad_pre).astype(bf)
    outer_grad = dot_tn(grad_mine, inner_act).astype(bf)
    weight_back = lax.all_to_all(
        jnp.stack(
            [
                inner_grad.reshape(group_count, width_share, hidden_share),
                outer_grad.reshape(group_count, width_share, hidden_share),
            ],
            axis=1,
        ),
        "dp",
        split_axis=0,
        concat_axis=0,
        tiled=True,
    )
    weight_sum = jnp.sum(
        weight_back.reshape(
            expert_count, serve_count, 2, width_share, hidden_share
        ).astype(jnp.float32),
        axis=1,
    )
    inner_sum = weight_sum[:, 0]
    outer_sum = weight_sum[:, 1].transpose(0, 2, 1)
    gate_local = lax.dynamic_slice_in_dim(gate_value, my_start, local_rows, 0)
    layer_out = (middle + gate_local[:, None] * expert_local).astype(bf)
    cot_local = cotangent.astype(jnp.float32)
    gate_grad = jnp.sum(cot_local * expert_local, axis=-1)
    probs_local = lax.dynamic_slice_in_dim(gate_probs, my_start, local_rows, 0)
    chosen_local = lax.dynamic_slice_in_dim(chosen.astype(jnp.float32), my_start, local_rows, 0)
    grad_logits = (probs_local * gate_grad[:, None] * (chosen_local - gate_local[:, None])).astype(
        jnp.bfloat16
    )
    grad_router_part = jnp.einsum(
        "qd,qe->de", normed_local, grad_logits, preferred_element_type=jnp.float32
    )
    router_term = jnp.einsum(
        "qe,de->qd", grad_logits, router_full, preferred_element_type=jnp.float32
    )
    grad_two_local = slots_local + router_term
    grad_mid, grad_gain_two = norm_backward(grad_two_local, middle, scale_two, gain_expert)
    grad_middle = cot_local + grad_mid
    (grad_mid_full,) = exchange(7, [(grad_middle.astype(bf), "tensor", "line")])
    grad_mid_full = grad_mid_full.reshape(group_rows, model_width)
    grad_out_w = dot_tn(grad_mid_full, mixed_all)
    grad_qkv, grad_one_sent, diagonals = pl.pallas_call(
        functools.partial(attend_back_kernel, head_width),
        out_shape=[
            jax.ShapeDtypeStruct((group_rows, 3 * head_width), bf),
            jax.ShapeDtypeStruct((group_rows, model_width), bf),
            jax.ShapeDtypeStruct((head_count, 8, 2 * group_rows), jnp.float32),
        ],
        in_specs=[vmem_block] * 4,
        out_specs=[vmem_block] * 3,
        scratch_shapes=[pltpu.VMEM((group_rows, 2 * group_rows), jnp.float32)],
        compiler_params=pltpu.CompilerParams(vmem_limit_bytes=vmem_bytes),
    )(grad_mid_full, attn_full, projected, probs)
    grad_rel_local = jnp.einsum(
        "hrt,brt->bh", diagonals, onehot, precision=lax.Precision.HIGHEST
    )
    grad_rel_full = lax.dynamic_update_slice_in_dim(
        jnp.zeros(rel_bias.shape, jnp.float32), grad_rel_local, head_start, 1
    )
    grad_qkv_w = dot_tn(normed_one, grad_qkv)
    attn_grads = jnp.concatenate([grad_qkv_w, grad_out_w], axis=1).astype(bf)
    grad_one_local, attn_back_parts = line_sum(
        8,
        grad_one_sent.reshape(tensor_count, local_rows, model_width),
        "tensor",
        attn_grads.reshape(group_count, width_share, 4 * head_width),
        "dp",
    )
    grad_in_norm, grad_gain_one = norm_backward(grad_one_local, input_f, scale_one, gain_attn)
    grad_tokens = (grad_middle + grad_in_norm).astype(bf)
    small = jnp.concatenate(
        [
            grad_gain_one,
            grad_gain_two,
            grad_rel_full.reshape(-1),
            grad_router_part.T.reshape(-1),
        ]
    )
    small_size = small.shape[0]
    small_rows = (small_size + 1023) // 1024 * 8
    small = jnp.pad(small, (0, small_rows * 128 - small_size)).reshape(small_rows, 128)
    (small_parts,) = exchange(9, [(small, "tensor", "gather")])
    (small_parts,) = exchange(10, [(jnp.sum(small_parts, axis=0), "dp", "gather")])
    small_sum = jnp.sum(small_parts, axis=0).reshape(-1)
    gain_one_sum = small_sum[:model_width]
    gain_two_sum = small_sum[model_width : 2 * model_width]
    rel_end = 2 * model_width + rel_bias.size
    rel_sum = small_sum[2 * model_width : rel_end].reshape(rel_bias.shape)
    router_whole = small_sum[rel_end : rel_end + expert_count * model_width].reshape(
        expert_count, model_width
    )
    router_sum = lax.dynamic_slice_in_dim(
        router_whole, lax.axis_index("dp") * width_share, width_share, 1
    ).T
    attn_sum = sum_parts(attn_back_parts)
    query_sum, key_sum, value_sum = (
        attn_sum[:, part * head_width : (part + 1) * head_width] for part in range(3)
    )
    out_sum = attn_sum[:, 3 * head_width :].T
    return (
        layer_out,
        grad_tokens,
        query_sum,
        key_sum,
        value_sum,
        out_sum,
        gain_one_sum,
        gain_two_sum,
        rel_sum,
        router_sum,
        inner_sum,
        outer_sum,
    )


def solution(mesh):
    return jax.shard_map(
        body,
        mesh=mesh,
        in_specs=(
            P(("dp", "tensor"), None),
            P("dp"),
            P("dp", None),
            P(("dp", "tensor"), None),
            P("dp", "tensor"),
            P("dp", "tensor"),
            P("dp", "tensor"),
            P("tensor", "dp"),
            P(),
            P(),
            P(),
            P("dp", None),
            P(None, "dp", "tensor"),
            P(None, "tensor", "dp"),
        ),
        out_specs=(
            P(("dp", "tensor"), None),
            P(("dp", "tensor"), None),
            P("dp", "tensor"),
            P("dp", "tensor"),
            P("dp", "tensor"),
            P("tensor", "dp"),
            P(),
            P(),
            P(),
            P("dp", None),
            P(None, "dp", "tensor"),
            P(None, "tensor", "dp"),
        ),
        check_vma=False,
    )
```

```python
import functools

import jax
import jax.numpy as jnp
import numpy as np
from jax import lax
from jax.experimental import pallas as pl
from jax.experimental.pallas import tpu as pltpu
from jax.sharding import PartitionSpec as P

HEAD_DIM = 64
BUCKETS = 32
MAX_DIST = 128


norm_eps = 1e-06
masked_score = -1e30


def bucket_table(length, buckets, max_reach):
    half_count = buckets // 2
    exact_count = half_count // 2
    positions = np.arange(length)
    offset = positions[None, :] - positions[:, None]
    distance = np.abs(offset)
    far_bucket = exact_count + (
        np.log(np.maximum(distance, 1) / exact_count)
        / np.log(max_reach / exact_count)
        * (half_count - exact_count)
    ).astype(np.int64)
    far_bucket = np.minimum(far_bucket, half_count - 1)
    bucket = np.where(distance < exact_count, distance, far_bucket) + half_count * (offset > 0)
    return bucket.astype(np.int32)


def rms_scale(values):
    return lax.rsqrt(jnp.mean(values * values, axis=-1, keepdims=True) + norm_eps)


def gelu_tanh(values):
    return jax.nn.gelu(values, approximate=True)


pieces = 4
vmem_bytes = 48 * 1024 * 1024


def greet_line(barrier, axis, size):
    me = lax.axis_index(axis)
    for side, there in ((1, me < size - 1), (-1, me > 0)):

        @pl.when(there)
        def greet(side=side):
            pl.semaphore_signal(
                barrier,
                inc=1,
                device_id={axis: me + side},
                device_id_type=pl.DeviceIdType.MESH,
            )

    return (me < size - 1).astype(jnp.int32) + (me > 0).astype(jnp.int32)


def line_gather(axis, size, items):
    me = lax.axis_index(axis)
    rows = items[0][0].shape[0] // pieces

    def hop(item, way, step, piece):
        x_ref, out_ref, send_sem, recv_sem = item
        side = 1 - 2 * way
        block = me - side * step
        part = pl.ds(piece * rows, rows)
        return pltpu.make_async_remote_copy(
            src_ref=x_ref.at[part] if step == 0 else out_ref.at[block, part],
            dst_ref=out_ref.at[block, part],
            send_sem=send_sem.at[way, step, piece],
            recv_sem=recv_sem.at[way, step, piece],
            device_id={axis: me + side},
            device_id_type=pl.DeviceIdType.MESH,
        )

    def arrival(item, way, step, piece):
        x_ref, out_ref, send_sem, recv_sem = item
        side = 1 - 2 * way
        block = me - side * (step + 1)
        part = pl.ds(piece * rows, rows)
        return pltpu.make_async_remote_copy(
            src_ref=x_ref.at[part],
            dst_ref=out_ref.at[block, part],
            send_sem=send_sem.at[way, step, piece],
            recv_sem=recv_sem.at[way, step, piece],
            device_id={axis: me + side},
            device_id_type=pl.DeviceIdType.MESH,
        )

    def sends(way, step):
        if way == 0:
            return (me < size - 1) & (me >= step)
        return (me > 0) & (me + step <= size - 1)

    def receives(way, step):
        if way == 0:
            return me >= step + 1
        return me + step + 1 <= size - 1

    for step in range(size):
        for item in items:
            for piece in range(pieces):
                for way in range(2):
                    if step > 0:

                        @pl.when(receives(way, step - 1))
                        def landed(item=item, way=way, step=step, piece=piece):
                            arrival(item, way, step - 1, piece).wait_recv()

                    if step < size - 1:

                        @pl.when(sends(way, step))
                        def forward(item=item, way=way, step=step, piece=piece):
                            hop(item, way, step, piece).start()

    for step in range(size - 1):
        for item in items:
            for piece in range(pieces):
                for way in range(2):

                    @pl.when(sends(way, step))
                    def gone(item=item, way=way, step=step, piece=piece):
                        hop(item, way, step, piece).wait_send()


def greet_direct(barrier, axis, size):
    me = lax.axis_index(axis)
    for step in range(1, size):
        pl.semaphore_signal(
            barrier,
            inc=1,
            device_id={axis: lax.rem(me + step, size)},
            device_id_type=pl.DeviceIdType.MESH,
        )
    return size - 1


def start_swap(axis, size, x_ref, out_ref, send_sem, recv_sem):
    me = lax.axis_index(axis)
    copies = []
    for step in range(1, size):
        peer = lax.rem(me + step, size)
        copy = pltpu.make_async_remote_copy(
            src_ref=x_ref.at[peer],
            dst_ref=out_ref.at[me],
            send_sem=send_sem.at[step],
            recv_sem=recv_sem.at[step],
            device_id={axis: peer},
            device_id_type=pl.DeviceIdType.MESH,
        )
        copy.start()
        copies.append(copy)
    own = pltpu.make_async_copy(x_ref.at[me], out_ref.at[me], send_sem.at[0])
    own.start()
    return copies + [own]


def line_sum_kernel(axis, size, beside, *refs):
    x_ref = refs[0]
    if beside:
        other_ref, out_ref, other_out, got, going, send_sem, recv_sem, swap_send, swap_recv = refs[1:]
    else:
        out_ref, got, going, send_sem, recv_sem = refs[1:]
    me = lax.axis_index(axis)
    barrier = pltpu.get_barrier_semaphore()
    greeted = greet_line(barrier, axis, size)
    if beside:
        greeted += greet_direct(barrier, *beside)
    pl.semaphore_wait(barrier, greeted)
    rows = x_ref.shape[1] // pieces
    far = (me >= size // 2).astype(jnp.int32)

    def hop(way, dest, piece):
        part = pl.ds(piece * rows, rows)
        return pltpu.make_async_remote_copy(
            src_ref=going.at[way, dest, part],
            dst_ref=got.at[way, dest, part],
            send_sem=send_sem.at[way, dest, piece],
            recv_sem=recv_sem.at[way, dest, piece],
            device_id={axis: me + 1 - 2 * way},
            device_id_type=pl.DeviceIdType.MESH,
        )

    def before(way, dest):
        return (1 - 2 * way) * (dest - me) > 0

    def first(way):
        return me == (size - 1) * way

    copies = []
    for turn in range(2):
        way = far if turn == 0 else 1 - far
        for order in range(size - 1):
            dest = (size - 1 - order) * (1 - way) + order * way
            for piece in range(pieces):
                part = pl.ds(piece * rows, rows)

                @pl.when(before(way, dest) & first(way))
                def begin(way=way, dest=dest, part=part):
                    going[way, dest, part] = x_ref[dest, part]

                @pl.when(before(way, dest) & jnp.logical_not(first(way)))
                def add(way=way, dest=dest, part=part, piece=piece):
                    hop(way, dest, piece).wait_recv()
                    going[way, dest, part] = (
                        x_ref[dest, part].astype(jnp.float32)
                        + got[way, dest, part].astype(jnp.float32)
                    ).astype(jnp.bfloat16)

                @pl.when(before(way, dest))
                def send(way=way, dest=dest, piece=piece):
                    hop(way, dest, piece).start()

        if beside and turn == 0:
            copies = start_swap(*beside, other_ref, other_out, swap_send, swap_recv)

    out_ref[...] = x_ref[me].astype(jnp.float32)
    for way in range(2):

        @pl.when(jnp.logical_not(first(way)))
        def finish(way=way):
            for piece in range(pieces):
                hop(way, me, piece).wait_recv()
            out_ref[...] += got[way, me].astype(jnp.float32)

    for dest in range(size):
        for piece in range(pieces):
            for way in range(2):

                @pl.when(before(way, dest))
                def gone(way=way, dest=dest, piece=piece):
                    hop(way, dest, piece).wait_send()

    for copy in copies:
        copy.wait()


def line_sum(ident, x, axis, other=None, other_axis=None):
    size = lax.axis_size(axis)
    block = pl.BlockSpec(memory_space=pltpu.VMEM)
    place = pl.BlockSpec(memory_space=pl.ANY)
    out_shape = [jax.ShapeDtypeStruct(x.shape[1:], jnp.float32)]
    scratch = [
        pltpu.VMEM((2,) + x.shape, x.dtype),
        pltpu.VMEM((2,) + x.shape, x.dtype),
        pltpu.SemaphoreType.DMA((2, size, pieces)),
        pltpu.SemaphoreType.DMA((2, size, pieces)),
    ]
    beside = None
    extra = []
    if other is not None:
        beside = (other_axis, lax.axis_size(other_axis))
        extra = [other]
        out_shape.append(jax.ShapeDtypeStruct(other.shape, other.dtype))
        scratch += [pltpu.SemaphoreType.DMA((beside[1],)), pltpu.SemaphoreType.DMA((beside[1],))]
    return pl.pallas_call(
        functools.partial(line_sum_kernel, axis, size, beside),
        out_shape=out_shape,
        in_specs=[block] + [place] * len(extra),
        out_specs=[block] + [place] * len(extra),
        scratch_shapes=scratch,
        compiler_params=pltpu.CompilerParams(
            collective_id=ident, has_side_effects=True, vmem_limit_bytes=vmem_bytes
        ),
    )(x, *extra)


def attend_kernel(head_width, normed_ref, weights_ref, base_ref, doc_col, doc_row, proj_ref, prob_ref, mixed_ref, sent_ref, bias):
    rows = normed_ref.shape[0]
    proj_ref[...] = dot_nn(normed_ref[...], weights_ref[:, : 3 * head_width]).astype(jnp.bfloat16)
    same = doc_col[...] == doc_row[...]
    mixed = []
    for head in range(head_width // HEAD_DIM):
        query, key, value = (
            proj_ref[:, part * head_width + head * HEAD_DIM : part * head_width + (head + 1) * HEAD_DIM]
            for part in range(3)
        )
        base = base_ref[head]
        for block in range(rows // 8):
            turned = base if block == 0 else pltpu.roll(base, 8 * block, 1)
            bias[8 * block : 8 * block + 8, :] = turned[:, :rows]
        scores = jnp.where(same, dot_nt(query, key) + bias[...], masked_score)
        exps = jnp.exp(scores - jnp.max(scores, axis=-1, keepdims=True))
        probs = exps / jnp.sum(exps, axis=-1, keepdims=True)
        prob_ref[head] = probs
        mixed.append(dot_nn(probs.astype(jnp.bfloat16), value).astype(jnp.bfloat16))
    mixed_ref[...] = jnp.concatenate(mixed, axis=1)
    sent_ref[...] = dot_nt(
        mixed_ref[...], weights_ref[:, 3 * head_width : 4 * head_width]
    ).astype(jnp.bfloat16)


def attend_back_kernel(head_width, grad_ref, weights_ref, proj_ref, prob_ref, grads_ref, sent_ref, diag_ref, wide):
    rows = grad_ref.shape[0]
    grad_mixed = dot_nn(
        grad_ref[...], weights_ref[:, 3 * head_width : 4 * head_width]
    ).astype(jnp.bfloat16)
    grads = [[], [], []]
    wide[:, rows:] = jnp.zeros((rows, rows), jnp.float32)
    for head in range(head_width // HEAD_DIM):
        query, key, value = (
            proj_ref[:, part * head_width + head * HEAD_DIM : part * head_width + (head + 1) * HEAD_DIM]
            for part in range(3)
        )
        grad_head = grad_mixed[:, head * HEAD_DIM : (head + 1) * HEAD_DIM]
        probs = prob_ref[head]
        grad_probs = dot_nt(grad_head, value)
        row_dot = jnp.sum(probs * grad_probs, axis=-1, keepdims=True)
        grad_scores = (probs * (grad_probs - row_dot)).astype(jnp.bfloat16)
        grads[0].append(dot_nn(grad_scores, key).astype(jnp.bfloat16))
        grads[1].append(dot_tn(grad_scores, query).astype(jnp.bfloat16))
        grads[2].append(dot_tn(probs.astype(jnp.bfloat16), grad_head).astype(jnp.bfloat16))
        wide[:, :rows] = grad_scores.astype(jnp.float32)
        total = wide[0:8, :]
        for block in range(1, rows // 8):
            total = total + pltpu.roll(wide[8 * block : 8 * block + 8, :], 2 * rows - 8 * block, 1)
        diag_ref[head] = total
    grads_ref[...] = jnp.concatenate(grads[0] + grads[1] + grads[2], axis=1)
    sent_ref[...] = dot_nt(grads_ref[...], weights_ref[:, : 3 * head_width]).astype(jnp.bfloat16)


def bucket_onehot(length):
    spread = np.arange(2 * length)[None, :] - np.arange(8)[:, None]
    spread = (spread + length) % (2 * length) - length
    table = bucket_table(length, BUCKETS, MAX_DIST)
    line = np.concatenate([table[:, 0][::-1], table[0, 1:]])
    picked = line[np.clip(spread + length - 1, 0, 2 * length - 2)]
    return (picked[None] == np.arange(BUCKETS)[:, None, None]).astype(np.float32)


def exchange_kernel(plan, sizes, *refs):
    count = len(plan)
    ins, outs = refs[:count], refs[count : 2 * count]
    send_sem, recv_sem, own_sem, line_send, line_recv = refs[2 * count :]
    barrier = pltpu.get_barrier_semaphore()
    greeted = 0
    direct = {axis for axis, kind in plan if kind != "line"}
    for axis, size in sizes:
        me = lax.axis_index(axis)
        if axis not in direct:
            greeted += greet_line(barrier, axis, size)
            continue
        for step in range(1, size):
            pl.semaphore_signal(
                barrier,
                inc=1,
                device_id={axis: lax.rem(me + step, size)},
                device_id_type=pl.DeviceIdType.MESH,
            )
        greeted += size - 1
    pl.semaphore_wait(barrier, greeted)
    size_of = dict(sizes)
    copies = []
    for step in range(1, max(size_of.values())):
        for num, (axis, kind) in enumerate(plan):
            size = size_of[axis]
            if step >= size or kind == "line":
                continue
            me = lax.axis_index(axis)
            peer = lax.rem(me + step, size)
            copy = pltpu.make_async_remote_copy(
                src_ref=ins[num] if kind == "gather" else ins[num].at[peer],
                dst_ref=outs[num].at[me],
                send_sem=send_sem.at[num, step],
                recv_sem=recv_sem.at[num, step],
                device_id={axis: peer},
                device_id_type=pl.DeviceIdType.MESH,
            )
            copy.start()
            copies.append(copy)
    for num, (axis, kind) in enumerate(plan):
        me = lax.axis_index(axis)
        own = pltpu.make_async_copy(
            ins[num].at[me] if kind == "swap" else ins[num], outs[num].at[me], own_sem.at[num]
        )
        own.start()
        copies.append(own)
    lines = [num for num, (unused, kind) in enumerate(plan) if kind == "line"]
    if lines:
        line_gather(
            plan[lines[0]][0],
            size_of[plan[lines[0]][0]],
            [(ins[num], outs[num], line_send.at[num], line_recv.at[num]) for num in lines],
        )
    for copy in copies:
        copy.wait()


def exchange(ident, items):
    plan = tuple((axis, kind) for unused, axis, kind in items)
    axes = sorted({axis for axis, unused in plan})
    sizes = tuple((axis, lax.axis_size(axis)) for axis in axes)
    size_of = dict(sizes)
    shapes = [
        jax.ShapeDtypeStruct(
            ((size_of[axis],) + x.shape) if kind != "swap" else x.shape, x.dtype
        )
        for x, axis, kind in items
    ]
    most = max(size_of.values())
    return pl.pallas_call(
        functools.partial(exchange_kernel, plan, sizes),
        out_shape=shapes,
        in_specs=[pl.BlockSpec(memory_space=pl.ANY)] * len(items),
        out_specs=[pl.BlockSpec(memory_space=pl.ANY)] * len(items),
        scratch_shapes=[
            pltpu.SemaphoreType.DMA((len(items), most)),
            pltpu.SemaphoreType.DMA((len(items), most)),
            pltpu.SemaphoreType.DMA((len(items),)),
            pltpu.SemaphoreType.DMA((len(items), 2, most, pieces)),
            pltpu.SemaphoreType.DMA((len(items), 2, most, pieces)),
        ],
        compiler_params=pltpu.CompilerParams(collective_id=ident, has_side_effects=True),
    )(*[x for x, unused, unused2 in items])


def dot_nn(left, right):
    return jnp.dot(left, right, preferred_element_type=jnp.float32)


def dot_nt(left, right):
    return lax.dot_general(left, right, (((1,), (1,)), ((), ())), preferred_element_type=jnp.float32)


def dot_tn(left, right):
    return lax.dot_general(left, right, (((0,), (0,)), ((), ())), preferred_element_type=jnp.float32)


def sum_parts(parts):
    return jnp.sum(parts.astype(jnp.float32), axis=0)


def norm_backward(grad_out, inputs_in, scale_in, gain_vec):
    scaled = grad_out * gain_vec
    grad_in = scale_in * scaled - inputs_in * scale_in**3 * jnp.mean(
        scaled * inputs_in, axis=-1, keepdims=True
    )
    grad_gain = jnp.sum(grad_out * inputs_in * scale_in, axis=0)
    return (grad_in, grad_gain)


def body(
    tokens,
    doc_ids,
    expert_ids,
    cotangent,
    w_query,
    w_key,
    w_value,
    w_attn_out,
    gain_attn,
    gain_expert,
    rel_bias,
    w_router,
    w_expert_in,
    w_expert_out,
):
    tensor_count = lax.axis_size("tensor")
    group_count = lax.axis_size("dp")
    local_rows = tokens.shape[0]
    group_rows = local_rows * tensor_count
    model_width = tokens.shape[1]
    width_share = model_width // group_count
    my_start = lax.axis_index("tensor") * local_rows
    expert_count = w_router.shape[1]
    serve_count = group_count // expert_count
    base_slots = 9 * group_rows // (8 * expert_count)
    capacity = (base_slots + serve_count - 1) // serve_count * serve_count
    slot_count = expert_count * capacity
    share_rows = capacity // serve_count
    share_pad = (share_rows + 15) // 16 * 16
    head_width = w_query.shape[1]
    head_count = head_width // HEAD_DIM
    bf = jnp.bfloat16
    sent_attn = jnp.concatenate(
        [
            w_query,
            w_key,
            w_value,
            w_attn_out.T,
            jnp.pad(w_router, ((0, 0), (0, 128 - expert_count))),
        ],
        axis=1,
    )
    sent_experts = jnp.repeat(
        jnp.stack([w_expert_in, w_expert_out.transpose(0, 2, 1)], axis=1), serve_count, axis=0
    )
    hidden_share = w_expert_in.shape[2]
    head_start = lax.axis_index("tensor") * head_count
    rel_local = lax.dynamic_slice_in_dim(rel_bias, head_start, head_count, 1)
    route_ids = expert_ids[:, 0]
    input_f = tokens.astype(jnp.float32)
    scale_one = rms_scale(input_f)
    sent_one = (input_f * scale_one * gain_attn).astype(bf)
    normed_parts, attn_parts, grad_full = exchange(
        1,
        [
            (sent_one, "tensor", "line"),
            (sent_attn, "dp", "gather"),
            (cotangent, "tensor", "line"),
        ],
    )
    grad_full = grad_full.reshape(group_rows, model_width)
    sent_experts, normed_parts = lax.optimization_barrier((sent_experts, normed_parts))
    expert_parts = lax.all_to_all(sent_experts, "dp", split_axis=0, concat_axis=0, tiled=True)
    normed_one = normed_parts.reshape(group_rows, model_width)
    attn_full = attn_parts.reshape(model_width, sent_attn.shape[1])
    router_full = attn_full[:, 4 * head_width : 4 * head_width + expert_count]
    onehot = jnp.asarray(bucket_onehot(group_rows))
    rel_base = jnp.einsum(
        "bh,brt->hrt", rel_local, onehot, precision=lax.Precision.HIGHEST
    )
    vmem_block = pl.BlockSpec(memory_space=pltpu.VMEM)
    projected, probs, mixed_all, attn_sent = pl.pallas_call(
        functools.partial(attend_kernel, head_width),
        out_shape=[
            jax.ShapeDtypeStruct((group_rows, 3 * head_width), bf),
            jax.ShapeDtypeStruct((head_count, group_rows, group_rows), jnp.float32),
            jax.ShapeDtypeStruct((group_rows, head_width), bf),
            jax.ShapeDtypeStruct((group_rows, model_width), bf),
        ],
        in_specs=[vmem_block] * 5,
        out_specs=[vmem_block] * 4,
        scratch_shapes=[pltpu.VMEM((group_rows, group_rows), jnp.float32)],
        compiler_params=pltpu.CompilerParams(vmem_limit_bytes=vmem_bytes),
    )(normed_one, attn_full, rel_base, doc_ids[:, None], doc_ids[None, :])
    (attn_sum_local,) = line_sum(
        2, attn_sent.reshape(tensor_count, local_rows, model_width), "tensor"
    )
    chosen = route_ids[:, None] == jnp.arange(expert_count)[None, :]
    earlier = jnp.asarray(np.tril(np.ones((group_rows, group_rows), np.float32), -1), bf)
    counts = dot_nn(earlier, chosen.astype(bf))
    slot_index = jnp.sum(jnp.where(chosen, counts, 0.0), axis=-1).astype(jnp.int32)
    server = route_ids * serve_count + slot_index // share_rows
    slot_place = server * share_pad + slot_index % share_rows
    place = (
        slot_place[None, :] == jnp.arange(group_count * share_pad, dtype=jnp.int32)[:, None]
    ).astype(bf)
    grad_slots = dot_nn(place, grad_full).astype(bf)
    middle = input_f + attn_sum_local
    scale_two = rms_scale(middle)
    normed_local = (middle * scale_two * gain_expert).astype(bf)
    normed_two, recv_grad = exchange(
        3,
        [
            (normed_local, "tensor", "line"),
            (grad_slots.reshape(group_count, share_pad, model_width), "dp", "swap"),
        ],
    )
    normed_two = normed_two.reshape(group_rows, model_width)
    logits = dot_nn(normed_two, router_full)
    gate_probs = jax.nn.softmax(logits, axis=-1)
    gate_value = jnp.sum(jnp.where(chosen, gate_probs, 0.0), axis=-1)
    gate_slots = jnp.sum(jnp.where(place > 0, gate_value[None, :], 0.0), axis=1)
    sent_rows = dot_nn(place, normed_two).astype(bf)
    recv_rows, recv_gate = exchange(
        4,
        [
            (sent_rows.reshape(group_count, share_pad, model_width), "dp", "swap"),
            (gate_slots.reshape(group_count, 1, share_pad), "dp", "swap"),
        ],
    )
    rows_mine = recv_rows.reshape(group_count * share_pad, model_width)
    grad_mine = (
        (recv_gate.reshape(group_count, share_pad, 1) * recv_grad.astype(jnp.float32))
        .astype(bf)
        .reshape(group_count * share_pad, model_width)
    )
    inner_mine = expert_parts[:, 0].reshape(model_width, hidden_share)
    outer_mine = expert_parts[:, 1].reshape(model_width, hidden_share)
    inner_pre = dot_nn(rows_mine, inner_mine)
    inner_act, gelu_pull = jax.vjp(gelu_tanh, inner_pre)
    inner_act = inner_act.astype(bf)
    expert_part = dot_nt(inner_act, outer_mine).astype(bf)
    grad_pre = gelu_pull(dot_nn(grad_mine, outer_mine))[0].astype(bf)
    grad_rows = dot_nt(grad_pre, inner_mine).astype(bf)
    (back_rows,) = exchange(
        5, [(expert_part.reshape(group_count, share_pad, model_width), "dp", "swap")]
    )
    returned = dot_tn(place, back_rows.reshape(group_count * share_pad, model_width)).astype(bf)
    expert_local, back_grads = line_sum(
        6,
        returned.reshape(tensor_count, local_rows, model_width),
        "tensor",
        grad_rows.reshape(group_count, share_pad, model_width),
        "dp",
    )
    inner_grad = dot_tn(rows_mine, grad_pre).astype(bf)
    outer_grad = dot_tn(grad_mine, inner_act).astype(bf)
    grads_returned = dot_tn(
        place, back_grads.reshape(group_count * share_pad, model_width)
    ).astype(bf)
    slots_local, inner_back = line_sum(
        11,
        grads_returned.reshape(tensor_count, local_rows, model_width),
        "tensor",
        inner_grad.reshape(group_count, width_share, hidden_share),
        "dp",
    )
    gate_local = lax.dynamic_slice_in_dim(gate_value, my_start, local_rows, 0)
    layer_out = (middle + gate_local[:, None] * expert_local).astype(bf)
    cot_local = cotangent.astype(jnp.float32)
    gate_grad = jnp.sum(cot_local * expert_local, axis=-1)
    probs_local = lax.dynamic_slice_in_dim(gate_probs, my_start, local_rows, 0)
    chosen_local = lax.dynamic_slice_in_dim(chosen.astype(jnp.float32), my_start, local_rows, 0)
    grad_logits = (probs_local * gate_grad[:, None] * (chosen_local - gate_local[:, None])).astype(
        jnp.bfloat16
    )
    grad_router_part = jnp.einsum(
        "qd,qe->de", normed_local, grad_logits, preferred_element_type=jnp.float32
    )
    router_term = jnp.einsum(
        "qe,de->qd", grad_logits, router_full, preferred_element_type=jnp.float32
    )
    grad_two_local = slots_local + router_term
    grad_mid, grad_gain_two = norm_backward(grad_two_local, middle, scale_two, gain_expert)
    grad_middle = cot_local + grad_mid
    grad_mid_full, outer_back = exchange(
        7,
        [
            (grad_middle.astype(bf), "tensor", "line"),
            (outer_grad.reshape(group_count, width_share, hidden_share), "dp", "swap"),
        ],
    )
    paired = (expert_count, serve_count, width_share, hidden_share)
    inner_sum = jnp.sum(inner_back.reshape(paired).astype(jnp.float32), axis=1)
    outer_sum = jnp.sum(outer_back.reshape(paired).astype(jnp.float32), axis=1).transpose(0, 2, 1)
    grad_mid_full = grad_mid_full.reshape(group_rows, model_width)
    grad_out_w = dot_tn(grad_mid_full, mixed_all)
    grad_qkv, grad_one_sent, diagonals = pl.pallas_call(
        functools.partial(attend_back_kernel, head_width),
        out_shape=[
            jax.ShapeDtypeStruct((group_rows, 3 * head_width), bf),
            jax.ShapeDtypeStruct((group_rows, model_width), bf),
            jax.ShapeDtypeStruct((head_count, 8, 2 * group_rows), jnp.float32),
        ],
        in_specs=[vmem_block] * 4,
        out_specs=[vmem_block] * 3,
        scratch_shapes=[pltpu.VMEM((group_rows, 2 * group_rows), jnp.float32)],
        compiler_params=pltpu.CompilerParams(vmem_limit_bytes=vmem_bytes),
    )(grad_mid_full, attn_full, projected, probs)
    grad_rel_local = jnp.einsum(
        "hrt,brt->bh", diagonals, onehot, precision=lax.Precision.HIGHEST
    )
    grad_rel_full = lax.dynamic_update_slice_in_dim(
        jnp.zeros(rel_bias.shape, jnp.float32), grad_rel_local, head_start, 1
    )
    grad_qkv_w = dot_tn(normed_one, grad_qkv)
    attn_grads = jnp.concatenate([grad_qkv_w, grad_out_w], axis=1).astype(bf)
    grad_one_local, attn_back_parts = line_sum(
        8,
        grad_one_sent.reshape(tensor_count, local_rows, model_width),
        "tensor",
        attn_grads.reshape(group_count, width_share, 4 * head_width),
        "dp",
    )
    grad_in_norm, grad_gain_one = norm_backward(grad_one_local, input_f, scale_one, gain_attn)
    grad_tokens = (grad_middle + grad_in_norm).astype(bf)
    small = jnp.concatenate(
        [
            grad_gain_one,
            grad_gain_two,
            grad_rel_full.reshape(-1),
            grad_router_part.T.reshape(-1),
        ]
    )
    small_size = small.shape[0]
    small_rows = (small_size + 1023) // 1024 * 8
    small = jnp.pad(small, (0, small_rows * 128 - small_size)).reshape(small_rows, 128)
    (small_parts,) = exchange(9, [(small, "tensor", "gather")])
    (small_parts,) = exchange(10, [(jnp.sum(small_parts, axis=0), "dp", "gather")])
    small_sum = jnp.sum(small_parts, axis=0).reshape(-1)
    gain_one_sum = small_sum[:model_width]
    gain_two_sum = small_sum[model_width : 2 * model_width]
    rel_end = 2 * model_width + rel_bias.size
    rel_sum = small_sum[2 * model_width : rel_end].reshape(rel_bias.shape)
    router_whole = small_sum[rel_end : rel_end + expert_count * model_width].reshape(
        expert_count, model_width
    )
    router_sum = lax.dynamic_slice_in_dim(
        router_whole, lax.axis_index("dp") * width_share, width_share, 1
    ).T
    attn_sum = sum_parts(attn_back_parts)
    query_sum, key_sum, value_sum = (
        attn_sum[:, part * head_width : (part + 1) * head_width] for part in range(3)
    )
    out_sum = attn_sum[:, 3 * head_width :].T
    return (
        layer_out,
        grad_tokens,
        query_sum,
        key_sum,
        value_sum,
        out_sum,
        gain_one_sum,
        gain_two_sum,
        rel_sum,
        router_sum,
        inner_sum,
        outer_sum,
    )


def solution(mesh):
    return jax.shard_map(
        body,
        mesh=mesh,
        in_specs=(
            P(("dp", "tensor"), None),
            P("dp"),
            P("dp", None),
            P(("dp", "tensor"), None),
            P("dp", "tensor"),
            P("dp", "tensor"),
            P("dp", "tensor"),
            P("tensor", "dp"),
            P(),
            P(),
            P(),
            P("dp", None),
            P(None, "dp", "tensor"),
            P(None, "tensor", "dp"),
        ),
        out_specs=(
            P(("dp", "tensor"), None),
            P(("dp", "tensor"), None),
            P("dp", "tensor"),
            P("dp", "tensor"),
            P("dp", "tensor"),
            P("tensor", "dp"),
            P(),
            P(),
            P(),
            P("dp", None),
            P(None, "dp", "tensor"),
            P(None, "tensor", "dp"),
        ),
        check_vma=False,
    )
```
